256 devices in a mesh: tmpl: 32 (over y, z_lo, core), img: 8 (over z_hi, x).
Axes of the slice: x: 4, y: 4, z: 8 (z_hi: 2, z_lo: 4; z = z_hi * 4 + z_lo), core: 2. Of those that a mesh axis runs over, the one named last changes fastest.
Arguments:
- images: bfloat16 [2048, 32768], P(('tmpl', 'img')), may hold values from -43 to 43
- ctf_ids: int32 [2048], P(('tmpl', 'img')), may hold values from 0 to 7
- cotangent: float32 [2048], P(('tmpl', 'img')), may hold values from -6 to 6
- templates: bfloat16 [2048, 32768], P('tmpl'), may hold values from -1 to 1
- template_orient: int32 [2048], P('tmpl'), may hold values from 0 to 511
- ctf_table: float32 [8, 32768], replicated, may hold values from 0.25 to 1
- log_prior: float32 [512], replicated, may hold values from -4 to 4
Outputs:
- template_grad: bfloat16 [2048, 32768], P('tmpl', 'img')
- loglik: float32 [2048], P(('tmpl', 'img'))
- prior_grad: float32 [512], replicated
The draws below stay inside these ranges and needn't reach their ends.
All inputs are finite; a program needn't handle non-finite values.
Results may differ from the reference program's by a relative error of at most 0.015.
Values may be sent and summed in bfloat16 or wider, within the bound.
A program may use at most 128 MiB of HBM per device.

```python
import math
import jax
import jax.numpy as jnp
from jax import lax

F = 32768
CLASSES = 8
ORIENTS = 512
IMG_DEV = 8
TEMPLATES = 2048
IMAGES = 2048
N_TMPL = 32
N_IMG = 8


def template_row(key, index):
    values = jax.random.normal(jax.random.fold_in(key, index), (F,), jnp.float32)
    return jnp.clip(values, -5.0, 5.0) / math.sqrt(F)


def draw_templates(key, part):
    rows = jax.vmap(lambda index: template_row(key, index))(jnp.arange(TEMPLATES, dtype=jnp.int32))
    return rows.astype(jnp.bfloat16)


def draw_images(key, part):
    key = jax.random.fold_in(key, 11)
    noise = jnp.clip(jax.random.normal(key, (IMAGES, F), jnp.float32), -5.0, 5.0)
    return noise.astype(jnp.bfloat16)


def set_ends(values, key, smallest, top_value):
    shape = values.shape
    index_at = [jax.random.randint(jax.random.fold_in(key, axis), (), 0, shape[axis]) for axis in range(len(shape))]
    values = values.at[tuple(index_at)].set(smallest)
    longest = shape.index(max(shape))
    index_at[longest] = (index_at[longest] + 1) % shape[longest]
    return values.at[tuple(index_at)].set(top_value)


def levels(stream_key, extent, cuts, smallest, largest):
    gain, own = 1.0, jax.random.fold_in(stream_key, 6)
    for position, parts in cuts:
        heights = jnp.exp(jax.random.uniform(jax.random.fold_in(own, position), (parts,), jnp.float32, smallest / len(cuts), largest / len(cuts)))
        gain = gain * jnp.repeat(heights, extent[position] // parts).reshape([-1 if axis == position else 1 for axis in range(len(extent))])
    return gain


def scatter_about(stream_key, shape, spread, most, shards=(), kind=jnp.bfloat16):
    drawn = spread * jax.random.normal(stream_key, shape, jnp.float32)
    if shards:
        drawn = drawn * levels(stream_key, shape, shards, -0.22, 0.18)
    return jnp.clip(drawn, -most, most).astype(kind)


def setup_inputs(seed: int = 0) -> dict:
    keys = jax.random.split(jax.random.key(seed), 8)
    return {
        "images": draw_images(jax.random.fold_in(keys[7], 71), 0),
        "ctf_ids": set_ends(jax.random.randint(keys[1], (IMAGES,), 0, CLASSES), jax.random.fold_in(keys[1], 1), 0, CLASSES - 1).astype(jnp.int32),
        "cotangent": scatter_about(keys[2], (IMAGES,), 1.0, 6.0, ((0, 256),), jnp.float32),
        "templates": draw_templates(jax.random.fold_in(keys[7], 71), 0),
        "template_orient": set_ends(jax.random.randint(keys[4], (TEMPLATES,), 0, ORIENTS), jax.random.fold_in(keys[4], 1), 0, ORIENTS - 1).astype(jnp.int32),
        "ctf_table": jnp.clip(jnp.exp(jax.random.uniform(keys[5], (CLASSES, F), jnp.float32, math.log(0.25), math.log(1.0))), 0.25, 1.0),
        "log_prior": scatter_about(keys[6], (ORIENTS,), 1.0, 4.0, (), jnp.float32),
    }


HIGH = lax.Precision.HIGHEST


def reference(images, ctf_ids, cotangent, templates, template_orient, ctf_table, log_prior):
    ctf_sq = ctf_table * ctf_table
    tmpl_wide = templates.astype(jnp.float32)
    norms = jnp.dot(ctf_sq, (tmpl_wide * tmpl_wide).T, precision=HIGH)
    orient_hot = (template_orient[:, None] == jnp.arange(ORIENTS, dtype=jnp.int32)[None, :]).astype(jnp.float32)
    prior_terms = jnp.dot(orient_hot, log_prior, precision=HIGH)
    class_hot = (ctf_ids[:, None] == jnp.arange(CLASSES, dtype=jnp.int32)[None, :]).astype(jnp.float32)
    image_ctf = jnp.dot(class_hot, ctf_table, precision=HIGH)
    weighted = (image_ctf * images.astype(jnp.float32)).astype(jnp.bfloat16)
    cot_round = cotangent.astype(jnp.bfloat16).astype(jnp.float32)
    group_rows = N_TMPL * IMG_DEV
    weighted_g = weighted.reshape(N_TMPL, N_IMG, IMG_DEV, F).transpose(1, 0, 2, 3).reshape(N_IMG, group_rows, F)
    hot_g = class_hot.reshape(N_TMPL, N_IMG, IMG_DEV, CLASSES).transpose(1, 0, 2, 3).reshape(N_IMG, group_rows, CLASSES)
    cot_g = cot_round.reshape(N_TMPL, N_IMG, IMG_DEV).transpose(1, 0, 2).reshape(N_IMG, group_rows)

    def one_group(carry, pieces):
        grad_sum, column_sum = carry
        wrows, hot, cot = pieces
        scores = jnp.dot(wrows, templates.T, preferred_element_type=jnp.float32)
        scores = scores - 0.5 * jnp.dot(hot, norms, precision=HIGH) + prior_terms[None, :]
        top = jnp.max(scores, axis=1)
        total = jnp.sum(jnp.exp(scores - top[:, None]), axis=1)
        loglik = top + jnp.log(total)
        probs = cot[:, None] * jnp.exp(scores - loglik[:, None])
        probs_b = probs.astype(jnp.bfloat16)
        direct = jnp.dot(probs_b.T, wrows, preferred_element_type=jnp.float32)
        class_weight = jnp.dot(probs_b.astype(jnp.float32).T, hot, precision=HIGH)
        partial_value = direct - tmpl_wide * jnp.dot(class_weight, ctf_sq, precision=HIGH)
        partial_value = partial_value.astype(jnp.bfloat16).astype(jnp.float32)
        return (grad_sum + partial_value, column_sum + jnp.sum(probs, axis=0)), loglik

    start = (jnp.zeros((TEMPLATES, F), jnp.float32), jnp.zeros((TEMPLATES,), jnp.float32))
    (grad_sum, column_sum), logliks = lax.scan(one_group, start, (weighted_g, hot_g, cot_g))
    loglik = logliks.reshape(N_IMG, N_TMPL, IMG_DEV).transpose(1, 0, 2).reshape(IMAGES)
    prior_grad = jnp.dot(column_sum, orient_hot, precision=HIGH)
    return grad_sum.astype(jnp.bfloat16), loglik, prior_grad
```

```python
import jax
import jax.numpy as jnp
from jax import lax
from jax.sharding import PartitionSpec as P

HIGH = lax.Precision.HIGHEST


def local(images, ctf_ids, cotangent, templates, template_orient, ctf_table, log_prior):
    classes = ctf_table.shape[0]
    orients = log_prior.shape[0]
    own_rows = images.shape[0]
    ctf_sq = ctf_table * ctf_table
    class_range = jnp.arange(classes, dtype=jnp.int32)
    own_hot = (ctf_ids[:, None] == class_range[None, :]).astype(jnp.float32)
    own_ctf = jnp.dot(own_hot, ctf_table, precision=HIGH)
    weighted = (own_ctf * images.astype(jnp.float32)).astype(jnp.bfloat16)
    cot_round = cotangent.astype(jnp.bfloat16).astype(jnp.float32)
    small = jnp.stack([ctf_ids.astype(jnp.float32), cot_round], axis=1)
    small = lax.all_gather(small, "tmpl", axis=0, tiled=True)
    weighted = lax.all_gather(weighted, "tmpl", axis=0, tiled=True)
    class_hot = (small[:, :1] == class_range[None, :].astype(jnp.float32)).astype(jnp.float32)
    cot_all = small[:, 1]
    tmpl_wide = templates.astype(jnp.float32)
    norms = jnp.dot(ctf_sq, (tmpl_wide * tmpl_wide).T, precision=HIGH)
    orient_hot = (template_orient[:, None] == jnp.arange(orients, dtype=jnp.int32)[None, :]).astype(
        jnp.float32
    )
    prior_terms = jnp.dot(orient_hot, log_prior, precision=HIGH)
    scores = jnp.einsum("if,jf->ij", weighted, templates, preferred_element_type=jnp.float32)
    scores = scores - 0.5 * jnp.dot(class_hot, norms, precision=HIGH) + prior_terms[None, :]
    local_top = jnp.max(scores, axis=1)
    local_sum = jnp.sum(jnp.exp(scores - local_top[:, None]), axis=1)
    stats = lax.all_gather(jnp.stack([local_top, local_sum]), "tmpl", axis=0)
    top = jnp.max(stats[:, 0], axis=0)
    total = jnp.sum(stats[:, 1] * jnp.exp(stats[:, 0] - top[None, :]), axis=0)
    loglik_all = top + jnp.log(total)
    probs = cot_all[:, None] * jnp.exp(scores - loglik_all[:, None])
    probs_b = probs.astype(jnp.bfloat16)
    prior_local = jnp.dot(jnp.sum(probs, axis=0), orient_hot, precision=HIGH)
    prior_grad = lax.psum(prior_local, ("tmpl", "img"))
    direct = jnp.einsum("ij,if->jf", probs_b, weighted, preferred_element_type=jnp.float32)
    class_weight = jnp.dot(probs_b.astype(jnp.float32).T, class_hot, precision=HIGH)
    partial_value = direct - tmpl_wide * jnp.dot(class_weight, ctf_sq, precision=HIGH)
    template_grad = lax.psum_scatter(
        partial_value.astype(jnp.bfloat16), "img", scatter_dimension=1, tiled=True
    )
    loglik = lax.dynamic_slice_in_dim(loglik_all, lax.axis_index("tmpl") * own_rows, own_rows)
    return (template_grad, loglik, prior_grad)


def solution(mesh):
    placed = (
        P(("tmpl", "img"), None),
        P(("tmpl", "img")),
        P(("tmpl", "img")),
        P("tmpl", None),
        P("tmpl"),
        P(),
        P(),
    )
    return jax.shard_map(
        local,
        mesh=mesh,
        in_specs=placed,
        out_specs=(P("tmpl", "img"), P(("tmpl", "img")), P()),
        check_vma=False,
    )
```

```python
import functools

import jax
import jax.numpy as jnp
from jax import lax
from jax.experimental import pallas as pl
from jax.experimental.pallas import tpu as pltpu
from jax.sharding import PartitionSpec as P

HIGH = lax.Precision.HIGHEST
MESH = pl.DeviceIdType.MESH
F32, BF16 = jnp.float32, jnp.bfloat16

Y, ZL, CORES, ZH, X = 4, 4, 2, 2, 4
A = 2
B = ZL // A
ZZ = ZH * A
K = A * CORES
PIECES = Y * B
FGROUP = ZZ * X * CORES

ORDER = (
    [(db, 0) for db in range(B)]
    + [(db, dy) for db in range(B) for dy in (1, 3)]
    + [(db, 2) for db in range(B)]
)
PIECE = {step: index for index, step in enumerate(ORDER)}
GROUPS = ((0, 3 * B), (3 * B, B))


def nt_dot(a, b, precision=None):
    return lax.dot_general(
        a, b, (((1,), (1,)), ((), ())), precision=precision, preferred_element_type=F32
    )


def tn_dot(a, b, precision=None):
    return lax.dot_general(
        a, b, (((0,), (0,)), ((), ())), precision=precision, preferred_element_type=F32
    )


def kernel(
    wsrc, templates, ctf, meta, tmeta, grad, loglik, prior,
    w, s, r1, r2, r3, t2, ctf_own, metas, tmetas, nz, nx, nc, cz, cx, cc, stats, bins,
    pall, p2, gout, sems,
):
    t, g = lax.axis_index("tmpl"), lax.axis_index("img")
    core, zl, y = t % CORES, (t // CORES) % ZL, t // (CORES * ZL)
    x, zh = g % X, g // X
    a, b = zl // B, zl % B
    zz = zh * A + a
    k = a * CORES + core
    rows, half = w.shape[-2], w.shape[-1]
    block = rows // 2
    cols = 2 * half
    depth, orient_rows = s.shape[-1], 4
    own_t = templates.shape[0]
    owned = PIECES * block

    def device(dy=0, db=0, dz=0, dx=0, dc=0):
        y2, b2, z2, x2, c2 = (y + dy) % Y, (b + db) % B, (zz + dz) % ZZ, (x + dx) % X, (core + dc) % CORES
        zl2 = (z2 % A) * B + b2
        return ((y2 * ZL + zl2) * CORES + c2, (z2 // A) * X + x2)

    def device_k(da, dc):
        a2, c2 = (a + da) % A, (core + dc) % CORES
        return ((y * ZL + a2 * B + b) * CORES + c2, g), a2 * CORES + c2

    used = [0]
    sent = []

    def take():
        used[0] += 1
        return sems.at[used[0] - 1]

    def remote(src, dst, dev):
        copy = pltpu.make_async_remote_copy(
            src_ref=src, dst_ref=dst, send_sem=take(), recv_sem=take(),
            device_id=dev, device_id_type=MESH,
        )
        copy.start()
        sent.append(copy)
        return copy

    def here(src, dst):
        copy = pltpu.make_async_copy(src, dst, take())
        copy.start()
        return copy

    ring_f = [(dz, dx, dc) for dz in range(ZZ) for dx in range(X) for dc in range(CORES)][1:]
    ring_p = ORDER[1:]
    ring_k = [(da, dc) for da in range(A) for dc in range(CORES)][1:]

    mine = pl.ds(pl.multiple_of((g * K + k) * cols, 128), cols)
    load_ctf = here(ctf.at[:, mine], ctf_own)
    load_t = [
        here(
            templates.at[:, pl.ds(pl.multiple_of((g * K + k) * cols + q * half, 128), half)],
            t2.at[q, k],
        )
        for q in range(2)
    ]
    barrier = pltpu.get_barrier_semaphore()
    for dz, dx, dc in ring_f:
        pl.semaphore_signal(barrier, inc=1, device_id=device(dz=dz, dx=dx, dc=dc), device_id_type=MESH)
    for db, dy in ring_p:
        pl.semaphore_signal(barrier, inc=1, device_id=device(dy=dy, db=db), device_id_type=MESH)
    pl.semaphore_wait(barrier, len(ring_f) + len(ring_p))

    exchange = {}
    z_order = sorted(range(ZZ), key=lambda dz: min(dz, ZZ - dz))
    own_copy = here(wsrc.at[g * K + k], w.at[0, 0, 0, 0])
    for dz in z_order:
        for dx in range(X):
            for dc in range(CORES):
                if (dz, dx, dc) == (0, 0, 0):
                    continue
                z2, x2, c2 = (zz + dz) % ZZ, (x + dx) % X, (core + dc) % CORES
                dest = ((z2 // A) * X + x2) * K + (z2 % A) * CORES + c2
                back = ((-dz) % ZZ, (-dc) % CORES, (-dx) % X)
                exchange.setdefault(back[0], []).append(
                    remote(wsrc.at[dest], w.at[0, back[0], back[1], back[2]], device(dz=dz, dx=dx, dc=dc))
                )
    exchange_t, exchange_tm = [], []
    for da, dc in ring_k:
        dev, k2 = device_k(da, dc)
        for q in range(2):
            start = pl.multiple_of((g * K + k2) * cols + q * half, 128)
            exchange_t.append(remote(templates.at[:, pl.ds(start, half)], t2.at[q, k], dev))
        exchange_tm.append(remote(tmeta, tmetas.at[k], dev))
    exchange_m = [
        remote(meta, metas.at[PIECE[((-db) % B, (-dy) % Y)]], device(dy=dy, db=db)) for db, dy in ring_p
    ]

    from_b, from_y = {}, {}

    def send_y(db, dz):
        piece = PIECE[(db, 0)]
        for step in (1, 3):
            from_y[(db, (-step) % Y, dz)] = remote(
                w.at[piece, dz], w.at[PIECE[(db, (-step) % Y)], dz], device(dy=step)
            )

    own_copy.wait()
    for dz in z_order:
        for copy in exchange[dz]:
            copy.wait_recv()
        for db in range(1, B):
            from_b[((-db) % B, dz)] = remote(
                w.at[0, dz], w.at[PIECE[((-db) % B, 0)], dz], device(db=db)
            )
        send_y(0, dz)

    load_ctf.wait()
    for copy in load_t:
        copy.wait()
    for copy in exchange_t + exchange_tm + exchange_m:
        copy.wait_recv()
    metas[0] = meta[...]
    tmetas[k] = tmeta[...]
    square = ctf_own[...] * ctf_own[...]
    norm_part = jnp.zeros((square.shape[0], depth), F32)
    for q in range(2):
        wide = t2[q].reshape(depth, half).astype(F32)
        norm_part += nt_dot(square[:, q * half : (q + 1) * half], wide * wide, HIGH)

    def sum_over(buffer, me, size, value, name):
        buffer[me] = value
        return [
            remote(buffer.at[me], buffer.at[me], device(**{name: step})) for step in range(1, size)
        ]

    def total_of(buffer, copies):
        for copy in copies:
            copy.wait_recv()
        total = buffer[0]
        for index in range(1, buffer.shape[0]):
            total = total + buffer[index]
        return total

    norm_copies = sum_over(nz, zz, ZZ, norm_part, "dz")

    def score(piece):
        lhs = w[piece].reshape(FGROUP * rows, half)
        out = nt_dot(lhs, t2[...].reshape(2 * depth, half))
        out = out.reshape(ZZ, CORES, X, 2, block, 2 * depth)
        value = out[:, :, :, 0, :, :depth] + out[:, :, :, 1, :, depth:]
        for dz in range(ZZ):
            for dc in range(CORES):
                for dx in range(X):
                    s[dc, dx, dz, piece] = value[dz, dc, dx]

    for db in range(1, B):
        for dz in z_order:
            from_b[(db, dz)].wait_recv()
            send_y(db, dz)
    norm_copies = sum_over(nx, x, X, total_of(nz, norm_copies), "dx")
    for db in range(B):
        score(PIECE[(db, 0)])

    far = {}
    for db in range(B):
        for dz in z_order:
            for side, step in ((0, 1), (1, 3)):
                source = (-step) % Y
                from_y[(db, source, dz)].wait_recv()
                far[(db, dz, side)] = remote(
                    w.at[PIECE[(db, source)], dz, side], w.at[PIECE[(db, 2)], dz, side], device(dy=step)
                )
    norm_copies = sum_over(nc, core, CORES, total_of(nx, norm_copies), "dc")

    def reduce_core(first, count):
        span = pl.ds(first, count)
        return remote(s.at[1, :, :, span], r1.at[:, :, span], device(dc=1))

    def reduce_x(first, count, copy):
        span = pl.ds(first, count)
        copy.wait_recv()
        s[0, :, :, span] = s[0, :, :, span] + r1[:, :, span]
        return [
            remote(s.at[0, dx, :, span], r2.at[dx - 1, :, span], device(dx=dx)) for dx in range(1, X)
        ]

    def reduce_z(first, count, copies):
        span = pl.ds(first, count)
        for copy in copies:
            copy.wait_recv()
        total = s[0, 0, :, span]
        for index in range(X - 1):
            total = total + r2[index, :, span]
        s[0, 0, :, span] = total
        return [
            remote(s.at[0, 0, dz, span], r3.at[dz - 1, span], device(dz=dz)) for dz in range(1, ZZ)
        ]

    for db in range(B):
        for dy in (1, 3):
            score(PIECE[(db, dy)])
    copies = reduce_core(*GROUPS[0])
    norms = total_of(nc, norm_copies)
    copies = reduce_x(*GROUPS[0], copies)
    for db in range(B):
        for dz in z_order:
            for side in range(2):
                far[(db, dz, side)].wait_recv()
        score(PIECE[(db, 2)])
    later = reduce_core(*GROUPS[1])
    copies = reduce_z(*GROUPS[0], copies)
    later = reduce_x(*GROUPS[1], later)
    later = reduce_z(*GROUPS[1], later)
    for copy in copies + later:
        copy.wait_recv()
    scores = s[0, 0, 0]
    for index in range(ZZ - 1):
        scores = scores + r3[index]
    scores = scores.reshape(owned, depth)

    info = metas[...].reshape(owned, 128)
    ids, cot = info[:, 0:1], info[:, 64:65]
    lane8 = lax.broadcasted_iota(jnp.int32, (1, 128), 1)
    prior_row = jnp.concatenate(
        [jnp.where(lane8 < 64, tmetas[i, 0:1, :], tmetas[i + 1, 0:1, :]) for i in range(0, K, 2)], axis=1
    )
    orient_row = jnp.concatenate(
        [jnp.where(lane8 < 64, tmetas[i, 1:2, :], tmetas[i + 1, 1:2, :]) for i in range(0, K, 2)], axis=1
    )
    norm_rows = jnp.zeros((owned, depth), F32)
    for c in range(norms.shape[0]):
        norm_rows = jnp.where(ids == float(c), norms[c : c + 1, :], norm_rows)
    scores = scores - 0.5 * norm_rows + prior_row
    top = jnp.max(scores, axis=1, keepdims=True)
    total = jnp.sum(jnp.exp(scores - top), axis=1, keepdims=True)
    sub = lax.broadcasted_iota(jnp.int32, (owned, 128), 0)
    lane = lax.broadcasted_iota(jnp.int32, (owned, 128), 1)
    target = sub % block
    for index, (db, dy) in enumerate(ORDER):
        place = ((y + dy) % Y) * B + (b + db) % B
        target = target + jnp.where(sub // block == index, place * block, 0)
    eye = target == lane
    sub8 = lax.broadcasted_iota(jnp.int32, (8, 128), 0)
    top_row = jnp.sum(jnp.where(eye, top, 0.0), axis=0, keepdims=True)
    total_row = jnp.sum(jnp.where(eye, total, 0.0), axis=0, keepdims=True)
    stats[0] = jnp.where(sub8 == 0, top_row, total_row)
    copies = [
        remote(stats.at[0], stats.at[PIECE[((-db) % B, (-dy) % Y)]], device(dy=dy, db=db)) for db, dy in ring_p
    ]
    for copy in copies:
        copy.wait_recv()
    best = stats[0, 0:1, :]
    for index in range(1, PIECES):
        best = jnp.maximum(best, stats[index, 0:1, :])
    full = jnp.zeros_like(best)
    for index in range(PIECES):
        full = full + stats[index, 1:2, :] * jnp.exp(stats[index, 0:1, :] - best)
    log_row = best + jnp.log(full)
    log_col = jnp.sum(jnp.where(eye, log_row, 0.0), axis=1, keepdims=True)
    loglik[...] = jnp.broadcast_to(log_col[0:block], (block, 128))
    probs = cot * jnp.exp(scores - log_col)
    rounded = probs.astype(BF16)
    pall[0, 0, 0] = rounded
    back = rounded.astype(F32)
    sums = [
        jnp.sum(jnp.where(ids == float(c), back, 0.0), axis=0, keepdims=True) for c in range(norms.shape[0])
    ]
    sums.append(jnp.broadcast_to(jnp.sum(probs, axis=0, keepdims=True), (8, depth)))

    copies = [
        remote(pall.at[0, 0, 0], pall.at[0, 0, (-dz) % ZZ], device(dz=dz)) for dz in range(1, ZZ)
    ]
    sum_copies = sum_over(cz, zz, ZZ, jnp.concatenate(sums, axis=0), "dz")
    for copy in copies:
        copy.wait_recv()
    copies = [remote(pall.at[0, 0], pall.at[0, (-dx) % X], device(dx=dx)) for dx in range(1, X)]
    sum_copies = sum_over(cx, x, X, total_of(cz, sum_copies), "dx")
    for copy in copies:
        copy.wait_recv()
    copies = [remote(pall.at[0], pall.at[1], device(dc=1))]
    sum_copies = sum_over(cc, core, CORES, total_of(cx, sum_copies), "dc")

    def expand(dc):
        for dx in range(X):
            for dz in range(ZZ):
                part = pall[dc, dx, dz].astype(F32).reshape(PIECES, block, depth)
                zero = jnp.zeros_like(part)
                left = jnp.concatenate([part, zero], axis=1)
                right = jnp.concatenate([zero, part], axis=1)
                p2[:, dz, dc, dx] = jnp.concatenate([left, right], axis=2).astype(BF16)

    expand(0)
    for copy in copies:
        copy.wait_recv()
    expand(1)
    sums = total_of(cc, sum_copies)
    column = sums[8:9, :]
    orients = 128 * orient_rows
    bin_id = lax.broadcasted_iota(jnp.int32, (orients, depth), 0).astype(F32)
    binned = jnp.sum(jnp.where(bin_id == orient_row, column, 0.0), axis=1, keepdims=True)
    eye128 = lax.broadcasted_iota(jnp.int32, (128, 128), 0) == lax.broadcasted_iota(jnp.int32, (128, 128), 1)
    tile = jnp.zeros((8, 128), F32)
    for index in range(orient_rows):
        part = binned[index * 128 : (index + 1) * 128]
        row = jnp.sum(jnp.where(eye128, part, 0.0), axis=0, keepdims=True)
        tile = jnp.where(sub8 == index, row, tile)
    place = y * B + b
    bins[place] = tile
    bin_copies = [remote(bins.at[place], bins.at[place], device(dy=dy, db=db)) for db, dy in ring_p]

    count = PIECES * FGROUP * rows
    direct = tn_dot(p2[...].reshape(count, 2 * depth), w[...].reshape(count, half))
    class_weight = sums[0:8, :]
    for q in range(2):
        correction = tn_dot(class_weight, square[:, q * half : (q + 1) * half], HIGH)
        wide = t2[q].reshape(depth, half).astype(F32)
        value = direct[q * depth : (q + 1) * depth] - wide * correction
        gout[q] = value.astype(BF16).reshape(K, own_t, half)
    copies, local = [], []
    for q in range(2):
        place_q = pl.ds(pl.multiple_of(k * cols + q * half, 128), half)
        local.append(here(gout.at[q, k], grad.at[:, place_q]))
        for da, dc in ring_k:
            dev, k2 = device_k(da, dc)
            copies.append(remote(gout.at[q, k2], grad.at[:, place_q], dev))
    prior[...] = total_of(bins, bin_copies)
    for copy in copies:
        copy.wait_recv()
    for copy in local:
        copy.wait()
    for copy in sent:
        copy.wait_send()


def local(images, ctf_ids, cotangent, templates, template_orient, ctf_table, log_prior):
    classes, width = ctf_table.shape
    orients = log_prior.shape[0]
    own_rows, own_t = images.shape[0], templates.shape[0]
    own_hot = (ctf_ids[:, None] == jnp.arange(classes, dtype=jnp.int32)[None, :]).astype(F32)
    own_ctf = jnp.dot(own_hot, ctf_table, precision=HIGH)
    weighted = (own_ctf * images.astype(F32)).astype(BF16)
    slices = ZH * X * K
    half = width // slices // 2
    rows = 2 * own_rows
    wsrc = weighted.reshape(own_rows, slices, 2, half).transpose(1, 2, 0, 3).reshape(slices, rows, half)
    cot = cotangent.astype(BF16).astype(F32)
    meta = jnp.concatenate(
        [
            jnp.broadcast_to(ctf_ids.astype(F32)[:, None], (own_rows, 64)),
            jnp.broadcast_to(cot[:, None], (own_rows, 64)),
        ],
        axis=1,
    )
    orient_hot = (template_orient[:, None] == jnp.arange(orients, dtype=jnp.int32)[None, :]).astype(F32)
    terms = jnp.dot(orient_hot, log_prior, precision=HIGH)
    tmeta = jnp.stack([terms, template_orient.astype(F32)])
    tmeta = jnp.pad(jnp.concatenate([tmeta, tmeta], axis=1), ((0, 6), (0, 0)))
    depth = K * own_t
    cols = 2 * half
    vmem, anywhere = pl.BlockSpec(memory_space=pltpu.VMEM), pl.BlockSpec(memory_space=pl.ANY)
    grad, loglik, prior = pl.pallas_call(
        kernel,
        out_shape=(
            jax.ShapeDtypeStruct((own_t, K * cols), BF16),
            jax.ShapeDtypeStruct((own_rows, 128), F32),
            jax.ShapeDtypeStruct((8, 128), F32),
        ),
        in_specs=[vmem, anywhere, anywhere, vmem, vmem],
        out_specs=(anywhere, vmem, vmem),
        scratch_shapes=[
            pltpu.VMEM((PIECES, ZZ, CORES, X, rows, half), BF16),
            pltpu.VMEM((CORES, X, ZZ, PIECES, own_rows, depth), F32),
            pltpu.VMEM((X, ZZ, PIECES, own_rows, depth), F32),
            pltpu.VMEM((X - 1, ZZ, PIECES, own_rows, depth), F32),
            pltpu.VMEM((ZZ - 1, PIECES, own_rows, depth), F32),
            pltpu.VMEM((2, K, own_t, half), BF16),
            pltpu.VMEM((classes, cols), F32),
            pltpu.VMEM((PIECES, own_rows, 128), F32),
            pltpu.VMEM((K, 8, 128), F32),
            pltpu.VMEM((ZZ, 8, depth), F32),
            pltpu.VMEM((X, 8, depth), F32),
            pltpu.VMEM((CORES, 8, depth), F32),
            pltpu.VMEM((ZZ, 16, depth), F32),
            pltpu.VMEM((X, 16, depth), F32),
            pltpu.VMEM((CORES, 16, depth), F32),
            pltpu.VMEM((PIECES, 8, 128), F32),
            pltpu.VMEM((PIECES, 8, 128), F32),
            pltpu.VMEM((CORES, X, ZZ, PIECES * own_rows, depth), BF16),
            pltpu.VMEM((PIECES, ZZ, CORES, X, rows, 2 * depth), BF16),
            pltpu.VMEM((2, K, own_t, half), BF16),
            pltpu.SemaphoreType.DMA((400,)),
        ],
        compiler_params=pltpu.CompilerParams(
            collective_id=0, has_side_effects=True, vmem_limit_bytes=50 * 1024 * 1024
        ),
        cost_estimate=pl.CostEstimate(flops=4 * 10**9, bytes_accessed=4 * 10**6, transcendentals=0),
    )(wsrc, templates, ctf_table, meta, tmeta)
    return grad, loglik[:, 0], prior[: orients // 128].reshape(orients)


def solution(mesh):
    placed = (
        P(("tmpl", "img"), None),
        P(("tmpl", "img")),
        P(("tmpl", "img")),
        P("tmpl", None),
        P("tmpl"),
        P(),
        P(),
    )
    return jax.shard_map(
        local,
        mesh=mesh,
        in_specs=placed,
        out_specs=(P("tmpl", "img"), P(("tmpl", "img")), P()),
        check_vma=False,
    )
```

```python
import functools

import jax
import jax.numpy as jnp
from jax import lax
from jax.experimental import pallas as pl
from jax.experimental.pallas import tpu as pltpu
from jax.sharding import PartitionSpec as P

HIGH = lax.Precision.HIGHEST
MESH = pl.DeviceIdType.MESH
F32, BF16 = jnp.float32, jnp.bfloat16

Y, ZL, CORES, ZH, X = 4, 4, 2, 2, 4
A = 2
B = ZL // A
ZZ = ZH * A
K = A * CORES
PIECES = Y * B
FGROUP = ZZ * X * CORES

ORDER = (
    [(db, 0) for db in range(B)]
    + [(db, dy) for db in range(B) for dy in (1, 3)]
    + [(db, 2) for db in range(B)]
)
PIECE = {step: index for index, step in enumerate(ORDER)}
Y_FIRST = ()
assert B == 2
GROUPS = (0, 2, 4, 6)


def nt_dot(a, b, precision=None):
    return lax.dot_general(
        a, b, (((1,), (1,)), ((), ())), precision=precision, preferred_element_type=F32
    )


def tn_dot(a, b, precision=None):
    return lax.dot_general(
        a, b, (((0,), (0,)), ((), ())), precision=precision, preferred_element_type=F32
    )


def column_of(row, size):
    wide = jnp.broadcast_to(row, (size, row.shape[1]))
    sub = lax.broadcasted_iota(jnp.int32, wide.shape, 0)
    lane = lax.broadcasted_iota(jnp.int32, wide.shape, 1)
    return jnp.sum(jnp.where(sub == lane, wide, 0.0), axis=1, keepdims=True)


def kernel(
    images, ids_hbm, cot_hbm, templates, orient_hbm, ctf, prior_hbm, grad, loglik, prior,
    own, table, ids_in, cot_in, orient_in, log_prior, cot_round, wsrc, w, s, r1, r2, r3, r4, t2, metas, tmetas, nz, nx, nc, cz, cx, cc, csum, stats, bins,
    pall, p2, gacc, gout, sems,
):
    t, g = lax.axis_index("tmpl"), lax.axis_index("img")
    core, zl, y = t % CORES, (t // CORES) % ZL, t // (CORES * ZL)
    x, zh = g % X, g // X
    a, b = zl // B, zl % B
    zz = zh * A + a
    k = a * CORES + core
    rows, half = w.shape[-2], w.shape[-1]
    block = rows // 2
    cols = 2 * half
    depth, orient_rows = s.shape[-1], 4
    own_t = templates.shape[0]
    owned = PIECES * block

    def device(dy=0, db=0, dz=0, dx=0, dc=0):
        y2, b2, z2, x2, c2 = (y + dy) % Y, (b + db) % B, (zz + dz) % ZZ, (x + dx) % X, (core + dc) % CORES
        zl2 = (z2 % A) * B + b2
        return ((y2 * ZL + zl2) * CORES + c2, (z2 // A) * X + x2)

    def device_k(da, dc):
        a2, c2 = (a + da) % A, (core + dc) % CORES
        return ((y * ZL + a2 * B + b) * CORES + c2, g), a2 * CORES + c2

    used = [0]
    sent = []

    def take():
        used[0] += 1
        return sems.at[used[0] - 1]

    def remote(src, dst, dev):
        copy = pltpu.make_async_remote_copy(
            src_ref=src, dst_ref=dst, send_sem=take(), recv_sem=take(),
            device_id=dev, device_id_type=MESH,
        )
        copy.start()
        sent.append(copy)
        return copy

    def here(src, dst):
        copy = pltpu.make_async_copy(src, dst, take())
        copy.start()
        return copy

    ring_f = [(dz, dx, dc) for dz in range(ZZ) for dx in range(X) for dc in range(CORES)][1:]
    ring_p = ORDER[1:]
    ring_k = [(da, dc) for da in range(A) for dc in range(CORES)][1:]

    load_own = [
        here(ids_hbm, ids_in), here(cot_hbm, cot_in), here(images, own), here(ctf, table),
        here(orient_hbm, orient_in), here(prior_hbm, log_prior),
    ]
    mine = pl.multiple_of((g * K + k) * cols, 128)
    load_t = [
        here(templates.at[:, pl.ds(pl.multiple_of(mine + q * half, 128), half)], t2.at[q, k])
        for q in range(2)
    ]
    barrier = pltpu.get_barrier_semaphore()
    for dz, dx, dc in ring_f:
        pl.semaphore_signal(barrier, inc=1, device_id=device(dz=dz, dx=dx, dc=dc), device_id_type=MESH)
    for db, dy in ring_p:
        pl.semaphore_signal(barrier, inc=1, device_id=device(dy=dy, db=db), device_id_type=MESH)
    for copy in load_own:
        copy.wait()

    ids_own = column_of(ids_in[...].astype(F32), block)
    cot_round[...] = jnp.broadcast_to(column_of(cot_in[...], block), cot_round.shape).astype(BF16)
    cot_own = cot_round[...].astype(F32)[:, 0:1]

    @pl.loop(0, wsrc.shape[0])
    def _(index):
        span = pl.ds(pl.multiple_of(index * cols, 128), cols)
        weight = jnp.broadcast_to(table[0:1, span], (block, cols))
        for c in range(1, table.shape[0]):
            weight = jnp.where(ids_own == float(c), table[c : c + 1, span], weight)
        value = weight * own[:, span].astype(F32)
        wsrc[index] = jnp.concatenate([value[:, :half], value[:, half:]], axis=0).astype(BF16)

    lane8 = lax.broadcasted_iota(jnp.int32, (block, 128), 1)
    metas[0] = jnp.where(lane8 < 64, ids_own, cot_own)
    pl.semaphore_wait(barrier, len(ring_f) + len(ring_p))

    exchange = {}
    z_order = sorted(range(ZZ), key=lambda dz: min(dz, ZZ - dz))
    own_copy = here(wsrc.at[g * K + k], w.at[0, 0, 0, 0])
    for dz in z_order:
        for dx in range(X):
            for dc in range(CORES):
                if (dz, dx, dc) == (0, 0, 0):
                    continue
                z2, x2, c2 = (zz + dz) % ZZ, (x + dx) % X, (core + dc) % CORES
                dest = ((z2 // A) * X + x2) * K + (z2 % A) * CORES + c2
                back = ((-dz) % ZZ, (-dc) % CORES, (-dx) % X)
                exchange.setdefault(back[0], []).append(
                    remote(wsrc.at[dest], w.at[0, back[0], back[1], back[2]], device(dz=dz, dx=dx, dc=dc))
                )

    from_b, from_y = {}, {}

    def send_y(db, dz):
        piece = PIECE[(db, 0)]
        for step in (1, 3):
            from_y[(db, (-step) % Y, dz)] = remote(
                w.at[piece, dz], w.at[PIECE[(db, (-step) % Y)], dz], device(dy=step)
            )

    own_copy.wait()
    for dz in z_order:
        for copy in exchange[dz]:
            copy.wait_recv()
        for db in range(1, B):
            from_b[((-db) % B, dz)] = remote(
                w.at[0, dz], w.at[PIECE[((-db) % B, 0)], dz], device(db=db)
            )
        send_y(0, dz)

    def sum_over(buffer, me, size, value, name):
        buffer[me] = value
        return [
            remote(buffer.at[me], buffer.at[me], device(**{name: step})) for step in range(1, size)
        ]

    def total_of(buffer, copies):
        for copy in copies:
            copy.wait_recv()
        total = buffer[0]
        for index in range(1, buffer.shape[0]):
            total = total + buffer[index]
        return total

    def reduce_core(first):
        span = pl.ds(first, B)
        return remote(s.at[1, :, :, span], r1.at[:, :, span], device(dc=1))

    def reduce_x(first, copy):
        span = pl.ds(first, B)
        copy.wait_recv()
        s[0, :, :, span] = s[0, :, :, span] + r1[:, :, span]
        return [
            remote(s.at[0, dx, :, span], r2.at[dx - 1, :, span], device(dx=dx)) for dx in range(1, X)
        ]

    def reduce_z(first, copies):
        span = pl.ds(first, B)
        for copy in copies:
            copy.wait_recv()
        total = s[0, 0, :, span]
        for index in range(X - 1):
            total = total + r2[index, :, span]
        s[0, 0, :, span] = total
        return [
            remote(s.at[0, 0, dz, span], r3.at[dz - 1, span], device(dz=dz)) for dz in range(1, ZZ)
        ]

    def score(piece):
        lhs = w[piece].reshape(FGROUP * rows, half)
        out = nt_dot(lhs, t2[...].reshape(2 * depth, half))
        out = out.reshape(ZZ, CORES, X, 2, block, 2 * depth)
        value = out[:, :, :, 0, :, :depth] + out[:, :, :, 1, :, depth:]
        for dz in range(ZZ):
            for dc in range(CORES):
                for dx in range(X):
                    s[dc, dx, dz, piece] = value[dz, dc, dx]

    orients = 128 * orient_rows
    orient_own = orient_in[...].astype(F32)
    orient_own = jnp.concatenate([orient_own, orient_own], axis=1)
    bin_id = lax.broadcasted_iota(jnp.int32, (orients, 128), 0).astype(F32)
    level = jnp.concatenate(
        [column_of(log_prior[index : index + 1, :], 128) for index in range(orient_rows)], axis=0
    )
    terms = jnp.sum(jnp.where(bin_id == orient_own, level, 0.0), axis=0, keepdims=True)
    sub8 = lax.broadcasted_iota(jnp.int32, (8, 128), 0)
    tmetas[k] = jnp.where(sub8 == 0, terms, orient_own)
    exchange_t, exchange_tm = [], []
    for da, dc in ring_k:
        dev, k2 = device_k(da, dc)
        for q in range(2):
            start = pl.multiple_of((g * K + k2) * cols + q * half, 128)
            exchange_t.append(remote(templates.at[:, pl.ds(start, half)], t2.at[q, k], dev))
        exchange_tm.append(remote(tmetas.at[k], tmetas.at[k], dev))
    exchange_m = [
        remote(metas.at[0], metas.at[PIECE[((-db) % B, (-dy) % Y)]], device(dy=dy, db=db)) for db, dy in ring_p
    ]

    far = {}

    def send_far(db, dz):
        for side, step in ((0, 1), (1, 3)):
            source = (-step) % Y
            from_y[(db, source, dz)].wait_recv()
            far[(db, dz, side)] = remote(
                w.at[PIECE[(db, source)], dz, side], w.at[PIECE[(db, 2)], dz, side], device(dy=step)
            )

    across = {}
    for dz in z_order:
        from_b[(1, dz)].wait_recv()
        if dz not in Y_FIRST:
            send_y(1, dz)
        send_far(0, dz)
        if dz in Y_FIRST:
            for dy in (1, 3):
                across[(dy, dz)] = remote(
                    w.at[PIECE[(0, dy)], dz], w.at[PIECE[(1, dy)], dz], device(db=1)
                )

    for copy in load_t:
        copy.wait()
    for copy in exchange_t + exchange_tm + exchange_m:
        copy.wait_recv()
    square = table[:, pl.ds(mine, cols)]
    square = square * square
    norm_part = jnp.zeros((square.shape[0], depth), F32)
    for q in range(2):
        wide = t2[q].reshape(depth, half).astype(F32)
        norm_part += nt_dot(square[:, q * half : (q + 1) * half], wide * wide, HIGH)
    norm_copies = sum_over(nz, zz, ZZ, norm_part, "dz")

    stage = [None] * len(GROUPS)
    for db in range(B):
        score(PIECE[(db, 0)])
    stage[0] = reduce_core(GROUPS[0])
    for dy in (1, 3):
        score(PIECE[(0, dy)])
    stage[0] = reduce_x(GROUPS[0], stage[0])
    stage[1] = reduce_core(GROUPS[1])
    norm_copies = sum_over(nx, x, X, total_of(nz, norm_copies), "dx")
    for dz in z_order:
        if dz not in Y_FIRST:
            send_far(1, dz)
    for dz in Y_FIRST:
        for side in range(2):
            far[(0, dz, side)].wait_recv()
        across[(2, dz)] = remote(w.at[PIECE[(0, 2)], dz], w.at[PIECE[(1, 2)], dz], device(db=1))
    stage[0] = reduce_z(GROUPS[0], stage[0])
    stage[1] = reduce_x(GROUPS[1], stage[1])
    norm_copies = sum_over(nc, core, CORES, total_of(nx, norm_copies), "dc")
    for dy in (1, 3):
        for dz in Y_FIRST:
            across[(dy, dz)].wait_recv()
        score(PIECE[(1, dy)])
    stage[2] = reduce_core(GROUPS[2])
    stage[1] = reduce_z(GROUPS[1], stage[1])
    stage[2] = reduce_x(GROUPS[2], stage[2])
    norms = total_of(nc, norm_copies)
    for db in range(B):
        for dz in z_order:
            if dz not in Y_FIRST:
                for side in range(2):
                    far[(db, dz, side)].wait_recv()
            elif db == 1:
                across[(2, dz)].wait_recv()
        score(PIECE[(db, 2)])
    stage[3] = reduce_core(GROUPS[3])
    stage[2] = reduce_z(GROUPS[2], stage[2])
    stage[3].wait_recv()
    span = pl.ds(GROUPS[3], B)
    s[0, :, :, span] = s[0, :, :, span] + r1[:, :, span]
    stage[3] = [
        remote(s.at[0, dx, dz, span], r4.at[dx * ZZ + dz - 1], device(dx=dx, dz=dz))
        for dz in range(ZZ) for dx in range(X) if (dx, dz) != (0, 0)
    ]
    for copies in stage:
        for copy in copies:
            copy.wait_recv()
    total = s[0, 0, 0, span]
    for index in range(X * ZZ - 1):
        total = total + r4[index]
    s[0, 0, 0, span] = total
    early = PIECES - B
    value = s[0, 0, 0, :early]
    for index in range(ZZ - 1):
        value = value + r3[index]
    s[0, 0, 0, :early] = value
    scores = s[0, 0, 0]
    scores = scores.reshape(owned, depth)

    info = metas[...].reshape(owned, 128)
    ids, cot = info[:, 0:1], info[:, 64:65]
    lane1 = lax.broadcasted_iota(jnp.int32, (1, 128), 1)
    prior_row = jnp.concatenate(
        [jnp.where(lane1 < 64, tmetas[i, 0:1, :], tmetas[i + 1, 0:1, :]) for i in range(0, K, 2)], axis=1
    )
    orient_row = jnp.concatenate(
        [jnp.where(lane1 < 64, tmetas[i, 1:2, :], tmetas[i + 1, 1:2, :]) for i in range(0, K, 2)], axis=1
    )
    norm_rows = jnp.zeros((owned, depth), F32)
    for c in range(norms.shape[0]):
        norm_rows = jnp.where(ids == float(c), norms[c : c + 1, :], norm_rows)
    scores = scores - 0.5 * norm_rows + prior_row
    top = jnp.max(scores, axis=1, keepdims=True)
    total = jnp.sum(jnp.exp(scores - top), axis=1, keepdims=True)
    sub = lax.broadcasted_iota(jnp.int32, (owned, 128), 0)
    lane = lax.broadcasted_iota(jnp.int32, (owned, 128), 1)
    target = sub % block
    for index, (db, dy) in enumerate(ORDER):
        place = ((y + dy) % Y) * B + (b + db) % B
        target = target + jnp.where(sub // block == index, place * block, 0)
    eye = target == lane
    top_row = jnp.sum(jnp.where(eye, top, 0.0), axis=0, keepdims=True)
    total_row = jnp.sum(jnp.where(eye, total, 0.0), axis=0, keepdims=True)
    stats[0] = jnp.where(sub8 == 0, top_row, total_row)
    copies = [
        remote(stats.at[0], stats.at[PIECE[((-db) % B, (-dy) % Y)]], device(dy=dy, db=db)) for db, dy in ring_p
    ]
    for copy in copies:
        copy.wait_recv()
    best = stats[0, 0:1, :]
    for index in range(1, PIECES):
        best = jnp.maximum(best, stats[index, 0:1, :])
    full = jnp.zeros_like(best)
    for index in range(PIECES):
        full = full + stats[index, 1:2, :] * jnp.exp(stats[index, 0:1, :] - best)
    log_row = best + jnp.log(full)
    log_col = jnp.sum(jnp.where(eye, log_row, 0.0), axis=1, keepdims=True)
    loglik[...] = jnp.broadcast_to(log_col[0:block], (block, 128))
    probs = cot * jnp.exp(scores - log_col)
    rounded = probs.astype(BF16)
    pall[0, 0, 0] = rounded

    def send_x(dz):
        return [
            remote(pall.at[0, 0, dz], pall.at[0, (-dx) % X, dz], device(dx=dx)) for dx in range(1, X)
        ]

    on_z = {
        (-dz) % ZZ: remote(pall.at[0, 0, 0], pall.at[0, 0, (-dz) % ZZ], device(dz=dz)) for dz in range(1, ZZ)
    }
    on_x = {0: send_x(0)}
    sums = [
        jnp.sum(jnp.where(ids == float(c), probs, 0.0), axis=0, keepdims=True) for c in range(norms.shape[0])
    ]
    sum_copies = sum_over(cz, zz, ZZ, jnp.concatenate(sums, axis=0), "dz")

    far_a = (a + 1) % A
    lanes = CORES * own_t

    def expand(dc, dz, side, which):
        span = pl.ds(pl.multiple_of(which * lanes, 128), lanes)
        for dx in range(X):
            part = pall[dc, dx, dz, :, span].astype(F32).reshape(PIECES, block, lanes)
            zero = jnp.zeros_like(part)
            left = jnp.concatenate([part, zero], axis=1)
            right = jnp.concatenate([zero, part], axis=1)
            p2[side, :, dx] = jnp.concatenate([left, right], axis=2).astype(BF16)

    def add_block(dc, dz, side, first=False):
        which = far_a if side == 0 else a
        expand(dc, dz, side, which)
        count = PIECES * X * rows
        value = tn_dot(p2[side].reshape(count, 2 * lanes), w[:, dz, dc].reshape(count, half))
        gacc[side] = value if first else gacc[side] + value

    for dz in z_order[1:]:
        on_z[dz].wait_recv()
        on_x[dz] = send_x(dz)
    sum_copies = sum_over(cx, x, X, total_of(cz, sum_copies), "dx")
    on_core = {}
    for dz in z_order:
        for copy in on_x[dz]:
            copy.wait_recv()
        on_core[dz] = remote(pall.at[0, :, dz], pall.at[1, :, dz], device(dc=1))
        if dz == z_order[0]:
            sum_copies = sum_over(cc, core, CORES, total_of(cx, sum_copies), "dc")
    for dz in z_order:
        add_block(0, dz, 0, dz == z_order[0])
    sums = total_of(cc, sum_copies)
    column = jnp.sum(sums, axis=0, keepdims=True)
    bin_id = lax.broadcasted_iota(jnp.int32, (orients, depth), 0).astype(F32)
    binned = jnp.sum(jnp.where(bin_id == orient_row, column, 0.0), axis=1, keepdims=True)
    eye128 = lax.broadcasted_iota(jnp.int32, (128, 128), 0) == lax.broadcasted_iota(jnp.int32, (128, 128), 1)
    tile = jnp.zeros((8, 128), F32)
    for index in range(orient_rows):
        part = binned[index * 128 : (index + 1) * 128]
        row = jnp.sum(jnp.where(eye128, part, 0.0), axis=0, keepdims=True)
        tile = jnp.where(sub8 == index, row, tile)
    place = y * B + b
    bins[place] = tile
    bin_copies = [remote(bins.at[place], bins.at[place], device(dy=dy, db=db)) for db, dy in ring_p]

    csum[...] = sums
    for dz in z_order:
        on_core[dz].wait_recv()
        add_block(1, dz, 0)
    copies, local = [], []
    for side in range(2):
        if side == 1:
            for dc in range(CORES):
                for dz in z_order:
                    add_block(dc, dz, 1, (dc, dz) == (0, z_order[0]))
        which = far_a if side == 0 else a
        span = pl.ds(pl.multiple_of(which * lanes, 128), lanes)
        class_weight = csum[:, span]
        for q in range(2):
            correction = tn_dot(class_weight, square[:, q * half : (q + 1) * half], HIGH)
            wide = t2[q, pl.ds(which * CORES, CORES)].reshape(lanes, half).astype(F32)
            value = gacc[side, q * lanes : (q + 1) * lanes] - wide * correction
            gout[side, q] = value.astype(BF16).reshape(CORES, own_t, half)
        for q in range(2):
            place_q = pl.ds(pl.multiple_of(k * cols + q * half, 128), half)
            for dc in range(CORES):
                dest = (core + dc) % CORES
                if (side, dc) == (1, 0):
                    local.append(here(gout.at[side, q, dest], grad.at[:, place_q]))
                else:
                    dev, _ = device_k(1 - side, dc)
                    copies.append(remote(gout.at[side, q, dest], grad.at[:, place_q], dev))
    prior[...] = total_of(bins, bin_copies)
    for copy in copies:
        copy.wait_recv()
    for copy in local:
        copy.wait()
    for copy in sent:
        copy.wait_send()


def local(images, ctf_ids, cotangent, templates, template_orient, ctf_table, log_prior):
    classes, width = ctf_table.shape
    orients = log_prior.shape[0]
    own_rows, own_t = images.shape[0], templates.shape[0]
    slices = ZH * X * K
    half = width // slices // 2
    rows = 2 * own_rows
    lanes = CORES * own_t
    depth = K * own_t
    cols = 2 * half
    vmem, anywhere = pl.BlockSpec(memory_space=pltpu.VMEM), pl.BlockSpec(memory_space=pl.ANY)
    grad, loglik, prior = pl.pallas_call(
        kernel,
        out_shape=(
            jax.ShapeDtypeStruct((own_t, K * cols), BF16),
            jax.ShapeDtypeStruct((own_rows, 128), F32),
            jax.ShapeDtypeStruct((8, 128), F32),
        ),
        in_specs=[pl.BlockSpec(memory_space=pltpu.HBM)] * 7,
        out_specs=(anywhere, vmem, vmem),
        scratch_shapes=[
            pltpu.VMEM((own_rows, width), BF16),
            pltpu.VMEM((classes, width), F32),
            pltpu.VMEM((1, own_rows), jnp.int32),
            pltpu.VMEM((1, own_rows), F32),
            pltpu.VMEM((1, own_t), jnp.int32),
            pltpu.VMEM((orients // 128, 128), F32),
            pltpu.VMEM((own_rows, 128), BF16),
            pltpu.VMEM((slices, rows, half), BF16),
            pltpu.VMEM((PIECES, ZZ, CORES, X, rows, half), BF16),
            pltpu.VMEM((CORES, X, ZZ, PIECES, own_rows, depth), F32),
            pltpu.VMEM((X, ZZ, PIECES, own_rows, depth), F32),
            pltpu.VMEM((X - 1, ZZ, PIECES - B, own_rows, depth), F32),
            pltpu.VMEM((ZZ - 1, PIECES - B, own_rows, depth), F32),
            pltpu.VMEM((X * ZZ - 1, B, own_rows, depth), F32),
            pltpu.VMEM((2, K, own_t, half), BF16),
            pltpu.VMEM((PIECES, own_rows, 128), F32),
            pltpu.VMEM((K, 8, 128), F32),
            pltpu.VMEM((ZZ, 8, depth), F32),
            pltpu.VMEM((X, 8, depth), F32),
            pltpu.VMEM((CORES, 8, depth), F32),
            pltpu.VMEM((ZZ, 8, depth), F32),
            pltpu.VMEM((X, 8, depth), F32),
            pltpu.VMEM((CORES, 8, depth), F32),
            pltpu.VMEM((8, depth), F32),
            pltpu.VMEM((PIECES, 8, 128), F32),
            pltpu.VMEM((PIECES, 8, 128), F32),
            pltpu.VMEM((CORES, X, ZZ, PIECES * own_rows, depth), BF16),
            pltpu.VMEM((2, PIECES, X, rows, 2 * lanes), BF16),
            pltpu.VMEM((2, 2 * lanes, half), F32),
            pltpu.VMEM((2, 2, CORES, own_t, half), BF16),
            pltpu.SemaphoreType.DMA((400,)),
        ],
        compiler_params=pltpu.CompilerParams(
            collective_id=0, has_side_effects=True, vmem_limit_bytes=56 * 1024 * 1024
        ),
        cost_estimate=pl.CostEstimate(flops=4 * 10**9, bytes_accessed=4 * 10**6, transcendentals=0),
    )(
        images,
        ctf_ids.reshape(1, own_rows),
        cotangent.reshape(1, own_rows),
        templates,
        template_orient.reshape(1, own_t),
        ctf_table,
        log_prior.reshape(orients // 128, 128),
    )
    return grad, loglik[:, 0], prior[: orients // 128].reshape(orients)


def solution(mesh):
    placed = (
        P(("tmpl", "img"), None),
        P(("tmpl", "img")),
        P(("tmpl", "img")),
        P("tmpl", None),
        P("tmpl"),
        P(),
        P(),
    )
    return jax.shard_map(
        local,
        mesh=mesh,
        in_specs=placed,
        out_specs=(P("tmpl", "img"), P(("tmpl", "img")), P()),
        check_vma=False,
    )
```

```python
import functools

import jax
import jax.numpy as jnp
from jax import lax
from jax.experimental import pallas as pl
from jax.experimental.pallas import tpu as pltpu
from jax.sharding import PartitionSpec as P

HIGH = lax.Precision.HIGHEST
MESH = pl.DeviceIdType.MESH
F32, BF16 = jnp.float32, jnp.bfloat16

Y, ZL, CORES, ZH, X = 4, 4, 2, 2, 4
A = 2
B = ZL // A
ZZ = ZH * A
K = A * CORES
PIECES = Y * B
FGROUP = ZZ * X * CORES

ORDER = (
    [(db, 0) for db in range(B)]
    + [(db, dy) for db in range(B) for dy in (1, 3)]
    + [(db, 2) for db in range(B)]
)
PIECE = {step: index for index, step in enumerate(ORDER)}
Y_FIRST = ()
assert B == 2
GROUPS = (0, 2, 4, 6)


def nt_dot(a, b, precision=None):
    return lax.dot_general(
        a, b, (((1,), (1,)), ((), ())), precision=precision, preferred_element_type=F32
    )


def tn_dot(a, b, precision=None):
    return lax.dot_general(
        a, b, (((0,), (0,)), ((), ())), precision=precision, preferred_element_type=F32
    )


def column_of(row, size):
    wide = jnp.broadcast_to(row, (size, row.shape[1]))
    sub = lax.broadcasted_iota(jnp.int32, wide.shape, 0)
    lane = lax.broadcasted_iota(jnp.int32, wide.shape, 1)
    return jnp.sum(jnp.where(sub == lane, wide, 0.0), axis=1, keepdims=True)


def kernel(
    images, ids_hbm, cot_hbm, templates, orient_hbm, ctf, prior_hbm, grad, loglik, prior,
    own, table, ids_in, cot_in, orient_in, log_prior, cot_round, wsrc, w, s, r1, r2, r3, r4, t2, metas, tmetas, nz, nx, nc, cz, cx, cc, csum, stats, bins,
    pall, p2, gacc, gout, sems,
):
    t, g = lax.axis_index("tmpl"), lax.axis_index("img")
    core, zl, y = t % CORES, (t // CORES) % ZL, t // (CORES * ZL)
    x, zh = g % X, g // X
    a, b = zl // B, zl % B
    zz = zh * A + a
    k = a * CORES + core
    rows, half = w.shape[-2], w.shape[-1]
    block = rows // 2
    cols = 2 * half
    depth, orient_rows = s.shape[-1], 4
    own_t = templates.shape[0]
    owned = PIECES * block

    def device(dy=0, db=0, dz=0, dx=0, dc=0):
        y2, b2, z2, x2, c2 = (y + dy) % Y, (b + db) % B, (zz + dz) % ZZ, (x + dx) % X, (core + dc) % CORES
        zl2 = (z2 % A) * B + b2
        return ((y2 * ZL + zl2) * CORES + c2, (z2 // A) * X + x2)

    def device_k(da, dc):
        a2, c2 = (a + da) % A, (core + dc) % CORES
        return ((y * ZL + a2 * B + b) * CORES + c2, g), a2 * CORES + c2

    used = [0]
    sent = []

    def take():
        used[0] += 1
        return sems.at[used[0] - 1]

    def remote(src, dst, dev):
        copy = pltpu.make_async_remote_copy(
            src_ref=src, dst_ref=dst, send_sem=take(), recv_sem=take(),
            device_id=dev, device_id_type=MESH,
        )
        copy.start()
        sent.append(copy)
        return copy

    def here(src, dst):
        copy = pltpu.make_async_copy(src, dst, take())
        copy.start()
        return copy

    ring_f = [(dz, dx, dc) for dz in range(ZZ) for dx in range(X) for dc in range(CORES)][1:]
    ring_p = ORDER[1:]
    ring_k = [(da, dc) for da in range(A) for dc in range(CORES)][1:]

    load_own = [
        here(ids_hbm, ids_in), here(cot_hbm, cot_in), here(images, own), here(ctf, table),
        here(orient_hbm, orient_in), here(prior_hbm, log_prior),
    ]
    mine = pl.multiple_of((g * K + k) * cols, 128)
    load_t = [
        here(templates.at[:, pl.ds(pl.multiple_of(mine + q * half, 128), half)], t2.at[q, k])
        for q in range(2)
    ]
    barrier = pltpu.get_barrier_semaphore()
    for dz, dx, dc in ring_f:
        pl.semaphore_signal(barrier, inc=1, device_id=device(dz=dz, dx=dx, dc=dc), device_id_type=MESH)
    for db, dy in ring_p:
        pl.semaphore_signal(barrier, inc=1, device_id=device(dy=dy, db=db), device_id_type=MESH)
    for copy in load_own:
        copy.wait()

    ids_own = column_of(ids_in[...].astype(F32), block)
    cot_round[...] = jnp.broadcast_to(column_of(cot_in[...], block), cot_round.shape).astype(BF16)
    cot_own = cot_round[...].astype(F32)[:, 0:1]

    @pl.loop(0, wsrc.shape[0])
    def _(index):
        span = pl.ds(pl.multiple_of(index * cols, 128), cols)
        weight = jnp.broadcast_to(table[0:1, span], (block, cols))
        for c in range(1, table.shape[0]):
            weight = jnp.where(ids_own == float(c), table[c : c + 1, span], weight)
        value = weight * own[:, span].astype(F32)
        wsrc[index] = jnp.concatenate([value[:, :half], value[:, half:]], axis=0).astype(BF16)

    lane8 = lax.broadcasted_iota(jnp.int32, (block, 128), 1)
    metas[0] = jnp.where(lane8 < 64, ids_own, cot_own)
    pl.semaphore_wait(barrier, len(ring_f) + len(ring_p))

    exchange = {}
    z_order = sorted(range(ZZ), key=lambda dz: min(dz, ZZ - dz))
    own_copy = here(wsrc.at[g * K + k], w.at[0, 0, 0, 0])
    for dz in z_order:
        for dx in range(X):
            for dc in range(CORES):
                if (dz, dx, dc) == (0, 0, 0):
                    continue
                z2, x2, c2 = (zz + dz) % ZZ, (x + dx) % X, (core + dc) % CORES
                dest = ((z2 // A) * X + x2) * K + (z2 % A) * CORES + c2
                back = ((-dz) % ZZ, (-dc) % CORES, (-dx) % X)
                exchange.setdefault(back[0], []).append(
                    remote(wsrc.at[dest], w.at[0, back[0], back[1], back[2]], device(dz=dz, dx=dx, dc=dc))
                )

    from_b, from_y = {}, {}

    def send_y(db, dz):
        piece = PIECE[(db, 0)]
        for step in (1, 3):
            from_y[(db, (-step) % Y, dz)] = remote(
                w.at[piece, dz], w.at[PIECE[(db, (-step) % Y)], dz], device(dy=step)
            )

    own_copy.wait()
    for dz in z_order:
        for copy in exchange[dz]:
            copy.wait_recv()
        for db in range(1, B):
            from_b[((-db) % B, dz)] = remote(
                w.at[0, dz], w.at[PIECE[((-db) % B, 0)], dz], device(db=db)
            )
        send_y(0, dz)

    def sum_over(buffer, me, size, value, name):
        buffer[me] = value
        return [
            remote(buffer.at[me], buffer.at[me], device(**{name: step})) for step in range(1, size)
        ]

    def total_of(buffer, copies):
        for copy in copies:
            copy.wait_recv()
        total = buffer[0]
        for index in range(1, buffer.shape[0]):
            total = total + buffer[index]
        return total

    def reduce_core(first):
        span = pl.ds(first, B)
        return remote(s.at[1, :, :, span], r1.at[:, :, span], device(dc=1))

    def reduce_x(first, copy):
        span = pl.ds(first, B)
        copy.wait_recv()
        s[0, :, :, span] = s[0, :, :, span] + r1[:, :, span]
        return [
            remote(s.at[0, dx, :, span], r2.at[dx - 1, :, span], device(dx=dx)) for dx in range(1, X)
        ]

    def reduce_z(first, copies):
        span = pl.ds(first, B)
        for copy in copies:
            copy.wait_recv()
        total = s[0, 0, :, span]
        for index in range(X - 1):
            total = total + r2[index, :, span]
        s[0, 0, :, span] = total
        return [
            remote(s.at[0, 0, dz, span], r3.at[dz - 1, span], device(dz=dz)) for dz in range(1, ZZ)
        ]

    def score(piece):
        lhs = w[piece].reshape(FGROUP * rows, half)
        out = nt_dot(lhs, t2[...].reshape(2 * depth, half))
        out = out.reshape(ZZ, CORES, X, 2, block, 2 * depth)
        value = out[:, :, :, 0, :, :depth] + out[:, :, :, 1, :, depth:]
        for dz in range(ZZ):
            for dc in range(CORES):
                for dx in range(X):
                    s[dc, dx, dz, piece] = value[dz, dc, dx]

    orients = 128 * orient_rows
    orient_own = orient_in[...].astype(F32)
    orient_own = jnp.concatenate([orient_own, orient_own], axis=1)
    bin_id = lax.broadcasted_iota(jnp.int32, (orients, 128), 0).astype(F32)
    level = jnp.concatenate(
        [column_of(log_prior[index : index + 1, :], 128) for index in range(orient_rows)], axis=0
    )
    terms = jnp.sum(jnp.where(bin_id == orient_own, level, 0.0), axis=0, keepdims=True)
    sub8 = lax.broadcasted_iota(jnp.int32, (8, 128), 0)
    tmetas[k] = jnp.where(sub8 == 0, terms, orient_own)
    exchange_t, exchange_tm = [], []
    for da, dc in ring_k:
        dev, k2 = device_k(da, dc)
        for q in range(2):
            start = pl.multiple_of((g * K + k2) * cols + q * half, 128)
            exchange_t.append(remote(templates.at[:, pl.ds(start, half)], t2.at[q, k], dev))
        exchange_tm.append(remote(tmetas.at[k], tmetas.at[k], dev))
    exchange_m = [
        remote(metas.at[0], metas.at[PIECE[((-db) % B, (-dy) % Y)]], device(dy=dy, db=db)) for db, dy in ring_p
    ]

    far = {}

    def send_far(db, dz):
        for side, step in ((0, 1), (1, 3)):
            source = (-step) % Y
            from_y[(db, source, dz)].wait_recv()
            far[(db, dz, side)] = remote(
                w.at[PIECE[(db, source)], dz, side], w.at[PIECE[(db, 2)], dz, side], device(dy=step)
            )

    across = {}
    for dz in z_order:
        from_b[(1, dz)].wait_recv()
        if dz not in Y_FIRST:
            send_y(1, dz)
        send_far(0, dz)
        if dz in Y_FIRST:
            for dy in (1, 3):
                across[(dy, dz)] = remote(
                    w.at[PIECE[(0, dy)], dz], w.at[PIECE[(1, dy)], dz], device(db=1)
                )

    for copy in load_t:
        copy.wait()
    for copy in exchange_t + exchange_tm + exchange_m:
        copy.wait_recv()
    square = table[:, pl.ds(mine, cols)]
    square = square * square
    norm_part = jnp.zeros((square.shape[0], depth), F32)
    for q in range(2):
        wide = t2[q].reshape(depth, half).astype(F32)
        norm_part += nt_dot(square[:, q * half : (q + 1) * half], wide * wide, HIGH)
    norm_copies = sum_over(nz, zz, ZZ, norm_part, "dz")

    stage = [None] * len(GROUPS)
    for db in range(B):
        score(PIECE[(db, 0)])
    stage[0] = reduce_core(GROUPS[0])
    for dy in (1, 3):
        score(PIECE[(0, dy)])
    stage[0] = reduce_x(GROUPS[0], stage[0])
    stage[1] = reduce_core(GROUPS[1])
    norm_copies = sum_over(nx, x, X, total_of(nz, norm_copies), "dx")
    for dz in z_order:
        if dz not in Y_FIRST:
            send_far(1, dz)
    for dz in Y_FIRST:
        for side in range(2):
            far[(0, dz, side)].wait_recv()
        across[(2, dz)] = remote(w.at[PIECE[(0, 2)], dz], w.at[PIECE[(1, 2)], dz], device(db=1))
    stage[1] = reduce_x(GROUPS[1], stage[1])
    stage[0] = reduce_z(GROUPS[0], stage[0])
    norm_copies = sum_over(nc, core, CORES, total_of(nx, norm_copies), "dc")
    for dy in (1, 3):
        for dz in Y_FIRST:
            across[(dy, dz)].wait_recv()
        score(PIECE[(1, dy)])
    stage[2] = reduce_core(GROUPS[2])
    stage[2] = reduce_x(GROUPS[2], stage[2])
    norms = total_of(nc, norm_copies)
    for db in range(B):
        for dz in z_order:
            if dz not in Y_FIRST:
                for side in range(2):
                    far[(db, dz, side)].wait_recv()
            elif db == 1:
                across[(2, dz)].wait_recv()
        score(PIECE[(db, 2)])
    stage[3] = reduce_core(GROUPS[3])
    stage[3].wait_recv()
    span = pl.ds(GROUPS[3], B)
    s[0, :, :, span] = s[0, :, :, span] + r1[:, :, span]
    stage[3] = [
        remote(s.at[0, dx, dz, span], r4.at[dx * ZZ + dz - 1], device(dx=dx, dz=dz))
        for dz in range(ZZ) for dx in range(X) if (dx, dz) != (0, 0)
    ]
    stage[1] = reduce_z(GROUPS[1], stage[1])
    stage[2] = reduce_z(GROUPS[2], stage[2])
    for copies in stage:
        for copy in copies:
            copy.wait_recv()
    total = s[0, 0, 0, span]
    for index in range(X * ZZ - 1):
        total = total + r4[index]
    s[0, 0, 0, span] = total
    early = PIECES - B
    value = s[0, 0, 0, :early]
    for index in range(ZZ - 1):
        value = value + r3[index]
    s[0, 0, 0, :early] = value
    scores = s[0, 0, 0]
    scores = scores.reshape(owned, depth)

    info = metas[...].reshape(owned, 128)
    ids, cot = info[:, 0:1], info[:, 64:65]
    lane1 = lax.broadcasted_iota(jnp.int32, (1, 128), 1)
    prior_row = jnp.concatenate(
        [jnp.where(lane1 < 64, tmetas[i, 0:1, :], tmetas[i + 1, 0:1, :]) for i in range(0, K, 2)], axis=1
    )
    orient_row = jnp.concatenate(
        [jnp.where(lane1 < 64, tmetas[i, 1:2, :], tmetas[i + 1, 1:2, :]) for i in range(0, K, 2)], axis=1
    )
    norm_rows = jnp.zeros((owned, depth), F32)
    for c in range(norms.shape[0]):
        norm_rows = jnp.where(ids == float(c), norms[c : c + 1, :], norm_rows)
    scores = scores - 0.5 * norm_rows + prior_row
    top = jnp.max(scores, axis=1, keepdims=True)
    total = jnp.sum(jnp.exp(scores - top), axis=1, keepdims=True)
    sub = lax.broadcasted_iota(jnp.int32, (owned, 128), 0)
    lane = lax.broadcasted_iota(jnp.int32, (owned, 128), 1)
    target = sub % block
    for index, (db, dy) in enumerate(ORDER):
        place = ((y + dy) % Y) * B + (b + db) % B
        target = target + jnp.where(sub // block == index, place * block, 0)
    eye = target == lane
    top_row = jnp.sum(jnp.where(eye, top, 0.0), axis=0, keepdims=True)
    total_row = jnp.sum(jnp.where(eye, total, 0.0), axis=0, keepdims=True)
    stats[0] = jnp.where(sub8 == 0, top_row, total_row)
    copies = [
        remote(stats.at[0], stats.at[PIECE[((-db) % B, (-dy) % Y)]], device(dy=dy, db=db)) for db, dy in ring_p
    ]
    for copy in copies:
        copy.wait_recv()
    best = stats[0, 0:1, :]
    for index in range(1, PIECES):
        best = jnp.maximum(best, stats[index, 0:1, :])
    full = jnp.zeros_like(best)
    for index in range(PIECES):
        full = full + stats[index, 1:2, :] * jnp.exp(stats[index, 0:1, :] - best)
    log_row = best + jnp.log(full)
    log_col = jnp.sum(jnp.where(eye, log_row, 0.0), axis=1, keepdims=True)
    loglik[...] = jnp.broadcast_to(log_col[0:block], (block, 128))
    probs = cot * jnp.exp(scores - log_col)
    rounded = probs.astype(BF16)
    pall[0, 0, 0] = rounded

    def send_x(dz):
        return [
            remote(pall.at[0, 0, dz], pall.at[0, (-dx) % X, dz], device(dx=dx)) for dx in range(1, X)
        ]

    on_z = {
        (-dz) % ZZ: remote(pall.at[0, 0, 0], pall.at[0, 0, (-dz) % ZZ], device(dz=dz)) for dz in range(1, ZZ)
    }
    on_x = {0: send_x(0)}
    sums = [
        jnp.sum(jnp.where(ids == float(c), probs, 0.0), axis=0, keepdims=True) for c in range(norms.shape[0])
    ]
    sum_copies = sum_over(cz, zz, ZZ, jnp.concatenate(sums, axis=0), "dz")

    far_a = (a + 1) % A
    lanes = CORES * own_t

    def expand(dc, dz, side, which):
        span = pl.ds(pl.multiple_of(which * lanes, 128), lanes)
        for dx in range(X):
            part = pall[dc, dx, dz, :, span].astype(F32).reshape(PIECES, block, lanes)
            zero = jnp.zeros_like(part)
            left = jnp.concatenate([part, zero], axis=1)
            right = jnp.concatenate([zero, part], axis=1)
            p2[side, :, dx] = jnp.concatenate([left, right], axis=2).astype(BF16)

    def add_block(dc, dz, side, first=False):
        which = far_a if side == 0 else a
        expand(dc, dz, side, which)
        count = PIECES * X * rows
        value = tn_dot(p2[side].reshape(count, 2 * lanes), w[:, dz, dc].reshape(count, half))
        gacc[side] = value if first else gacc[side] + value

    for dz in z_order[1:]:
        on_z[dz].wait_recv()
        on_x[dz] = send_x(dz)
    sum_copies = sum_over(cx, x, X, total_of(cz, sum_copies), "dx")
    on_core = {}
    for dz in z_order:
        for copy in on_x[dz]:
            copy.wait_recv()
        on_core[dz] = remote(pall.at[0, :, dz], pall.at[1, :, dz], device(dc=1))
        if dz == z_order[0]:
            sum_copies = sum_over(cc, core, CORES, total_of(cx, sum_copies), "dc")
    for dz in z_order:
        add_block(0, dz, 0, dz == z_order[0])
    sums = total_of(cc, sum_copies)
    column = jnp.sum(sums, axis=0, keepdims=True)
    bin_id = lax.broadcasted_iota(jnp.int32, (orients, depth), 0).astype(F32)
    binned = jnp.sum(jnp.where(bin_id == orient_row, column, 0.0), axis=1, keepdims=True)
    eye128 = lax.broadcasted_iota(jnp.int32, (128, 128), 0) == lax.broadcasted_iota(jnp.int32, (128, 128), 1)
    tile = jnp.zeros((8, 128), F32)
    for index in range(orient_rows):
        part = binned[index * 128 : (index + 1) * 128]
        row = jnp.sum(jnp.where(eye128, part, 0.0), axis=0, keepdims=True)
        tile = jnp.where(sub8 == index, row, tile)
    place = y * B + b
    bins[place] = tile
    bin_copies = [remote(bins.at[place], bins.at[place], device(dy=dy, db=db)) for db, dy in ring_p]

    csum[...] = sums
    for dz in z_order:
        on_core[dz].wait_recv()
        add_block(1, dz, 0)
    copies, local = [], []
    for side in range(2):
        if side == 1:
            for dc in range(CORES):
                for dz in z_order:
                    add_block(dc, dz, 1, (dc, dz) == (0, z_order[0]))
        which = far_a if side == 0 else a
        span = pl.ds(pl.multiple_of(which * lanes, 128), lanes)
        class_weight = csum[:, span]
        for q in range(2):
            correction = tn_dot(class_weight, square[:, q * half : (q + 1) * half], HIGH)
            wide = t2[q, pl.ds(which * CORES, CORES)].reshape(lanes, half).astype(F32)
            value = gacc[side, q * lanes : (q + 1) * lanes] - wide * correction
            gout[side, q] = value.astype(BF16).reshape(CORES, own_t, half)
        for q in range(2):
            place_q = pl.ds(pl.multiple_of(k * cols + q * half, 128), half)
            for dc in range(CORES):
                dest = (core + dc) % CORES
                if (side, dc) == (1, 0):
                    local.append(here(gout.at[side, q, dest], grad.at[:, place_q]))
                else:
                    dev, _ = device_k(1 - side, dc)
                    copies.append(remote(gout.at[side, q, dest], grad.at[:, place_q], dev))
    prior[...] = total_of(bins, bin_copies)
    for copy in copies:
        copy.wait_recv()
    for copy in local:
        copy.wait()
    for copy in sent:
        copy.wait_send()


def local(images, ctf_ids, cotangent, templates, template_orient, ctf_table, log_prior):
    classes, width = ctf_table.shape
    orients = log_prior.shape[0]
    own_rows, own_t = images.shape[0], templates.shape[0]
    slices = ZH * X * K
    half = width // slices // 2
    rows = 2 * own_rows
    lanes = CORES * own_t
    depth = K * own_t
    cols = 2 * half
    vmem, anywhere = pl.BlockSpec(memory_space=pltpu.VMEM), pl.BlockSpec(memory_space=pl.ANY)
    grad, loglik, prior = pl.pallas_call(
        kernel,
        out_shape=(
            jax.ShapeDtypeStruct((own_t, K * cols), BF16),
            jax.ShapeDtypeStruct((own_rows, 128), F32),
            jax.ShapeDtypeStruct((8, 128), F32),
        ),
        in_specs=[pl.BlockSpec(memory_space=pltpu.HBM)] * 7,
        out_specs=(anywhere, vmem, vmem),
        scratch_shapes=[
            pltpu.VMEM((own_rows, width), BF16),
            pltpu.VMEM((classes, width), F32),
            pltpu.VMEM((1, own_rows), jnp.int32),
            pltpu.VMEM((1, own_rows), F32),
            pltpu.VMEM((1, own_t), jnp.int32),
            pltpu.VMEM((orients // 128, 128), F32),
            pltpu.VMEM((own_rows, 128), BF16),
            pltpu.VMEM((slices, rows, half), BF16),
            pltpu.VMEM((PIECES, ZZ, CORES, X, rows, half), BF16),
            pltpu.VMEM((CORES, X, ZZ, PIECES, own_rows, depth), F32),
            pltpu.VMEM((X, ZZ, PIECES, own_rows, depth), F32),
            pltpu.VMEM((X - 1, ZZ, PIECES - B, own_rows, depth), F32),
            pltpu.VMEM((ZZ - 1, PIECES - B, own_rows, depth), F32),
            pltpu.VMEM((X * ZZ - 1, B, own_rows, depth), F32),
            pltpu.VMEM((2, K, own_t, half), BF16),
            pltpu.VMEM((PIECES, own_rows, 128), F32),
            pltpu.VMEM((K, 8, 128), F32),
            pltpu.VMEM((ZZ, 8, depth), F32),
            pltpu.VMEM((X, 8, depth), F32),
            pltpu.VMEM((CORES, 8, depth), F32),
            pltpu.VMEM((ZZ, 8, depth), F32),
            pltpu.VMEM((X, 8, depth), F32),
            pltpu.VMEM((CORES, 8, depth), F32),
            pltpu.VMEM((8, depth), F32),
            pltpu.VMEM((PIECES, 8, 128), F32),
            pltpu.VMEM((PIECES, 8, 128), F32),
            pltpu.VMEM((CORES, X, ZZ, PIECES * own_rows, depth), BF16),
            pltpu.VMEM((2, PIECES, X, rows, 2 * lanes), BF16),
            pltpu.VMEM((2, 2 * lanes, half), F32),
            pltpu.VMEM((2, 2, CORES, own_t, half), BF16),
            pltpu.SemaphoreType.DMA((400,)),
        ],
        compiler_params=pltpu.CompilerParams(
            collective_id=0, has_side_effects=True, vmem_limit_bytes=56 * 1024 * 1024
        ),
        cost_estimate=pl.CostEstimate(flops=4 * 10**9, bytes_accessed=4 * 10**6, transcendentals=0),
    )(
        images,
        ctf_ids.reshape(1, own_rows),
        cotangent.reshape(1, own_rows),
        templates,
        template_orient.reshape(1, own_t),
        ctf_table,
        log_prior.reshape(orients // 128, 128),
    )
    return grad, loglik[:, 0], prior[: orients // 128].reshape(orients)


def solution(mesh):
    placed = (
        P(("tmpl", "img"), None),
        P(("tmpl", "img")),
        P(("tmpl", "img")),
        P("tmpl", None),
        P("tmpl"),
        P(),
        P(),
    )
    return jax.shard_map(
        local,
        mesh=mesh,
        in_specs=placed,
        out_specs=(P("tmpl", "img"), P(("tmpl", "img")), P()),
        check_vma=False,
    )
```

```python
import functools

import jax
import jax.numpy as jnp
from jax import lax
from jax.experimental import pallas as pl
from jax.experimental.pallas import tpu as pltpu
from jax.sharding import PartitionSpec as P

HIGH = lax.Precision.HIGHEST
MESH = pl.DeviceIdType.MESH
F32, BF16 = jnp.float32, jnp.bfloat16

Y, ZL, CORES, ZH, X = 4, 4, 2, 2, 4
A = 2
B = ZL // A
ZZ = ZH * A
K = A * CORES
PIECES = Y * B
FGROUP = ZZ * X * CORES

ORDER = (
    [(db, 0) for db in range(B)]
    + [(db, dy) for db in range(B) for dy in (1, 3)]
    + [(db, 2) for db in range(B)]
)
PIECE = {step: index for index, step in enumerate(ORDER)}
Y_FIRST = ()
assert B == 2
GROUPS = (0, 2, 4, 6)


def nt_dot(a, b, precision=None):
    return lax.dot_general(
        a, b, (((1,), (1,)), ((), ())), precision=precision, preferred_element_type=F32
    )


def tn_dot(a, b, precision=None):
    return lax.dot_general(
        a, b, (((0,), (0,)), ((), ())), precision=precision, preferred_element_type=F32
    )


def column_of(row, size):
    wide = jnp.broadcast_to(row, (size, row.shape[1]))
    sub = lax.broadcasted_iota(jnp.int32, wide.shape, 0)
    lane = lax.broadcasted_iota(jnp.int32, wide.shape, 1)
    return jnp.sum(jnp.where(sub == lane, wide, 0.0), axis=1, keepdims=True)


def kernel(
    images, ids_hbm, cot_hbm, templates, orient_hbm, ctf, prior_hbm, grad, loglik, prior,
    own, table, ids_in, cot_in, orient_in, log_prior, cot_round, wsrc, w, s, r1, r2, r3, r4, t2, metas, tmetas, nz, nx, nc, cz, cx, cc, csum, stats, bins,
    pall, p2, gacc, gout, sems,
):
    t, g = lax.axis_index("tmpl"), lax.axis_index("img")
    core, zl, y = t % CORES, (t // CORES) % ZL, t // (CORES * ZL)
    x, zh = g % X, g // X
    a, b = zl // B, zl % B
    zz = zh * A + a
    k = a * CORES + core
    rows, half = w.shape[-2], w.shape[-1]
    block = rows // 2
    cols = 2 * half
    depth, orient_rows = s.shape[-1], 4
    own_t = templates.shape[0]
    owned = PIECES * block

    def device(dy=0, db=0, dz=0, dx=0, dc=0):
        y2, b2, z2, x2, c2 = (y + dy) % Y, (b + db) % B, (zz + dz) % ZZ, (x + dx) % X, (core + dc) % CORES
        zl2 = (z2 % A) * B + b2
        return ((y2 * ZL + zl2) * CORES + c2, (z2 // A) * X + x2)

    def device_k(da, dc):
        a2, c2 = (a + da) % A, (core + dc) % CORES
        return ((y * ZL + a2 * B + b) * CORES + c2, g), a2 * CORES + c2

    used = [0]
    sent = []

    def take():
        used[0] += 1
        return sems.at[used[0] - 1]

    def remote(src, dst, dev):
        copy = pltpu.make_async_remote_copy(
            src_ref=src, dst_ref=dst, send_sem=take(), recv_sem=take(),
            device_id=dev, device_id_type=MESH,
        )
        copy.start()
        sent.append(copy)
        return copy

    def here(src, dst):
        copy = pltpu.make_async_copy(src, dst, take())
        copy.start()
        return copy

    ring_f = [(dz, dx, dc) for dz in range(ZZ) for dx in range(X) for dc in range(CORES)][1:]
    ring_p = ORDER[1:]
    ring_k = [(da, dc) for da in range(A) for dc in range(CORES)][1:]

    load_own = [
        here(ids_hbm, ids_in), here(cot_hbm, cot_in), here(images, own), here(ctf, table),
        here(orient_hbm, orient_in), here(prior_hbm, log_prior),
    ]
    mine = pl.multiple_of((g * K + k) * cols, 128)
    load_t = [
        here(templates.at[:, pl.ds(pl.multiple_of(mine + q * half, 128), half)], t2.at[q, k])
        for q in range(2)
    ]
    barrier = pltpu.get_barrier_semaphore()
    for dz, dx, dc in ring_f:
        pl.semaphore_signal(barrier, inc=1, device_id=device(dz=dz, dx=dx, dc=dc), device_id_type=MESH)
    for db, dy in ring_p:
        pl.semaphore_signal(barrier, inc=1, device_id=device(dy=dy, db=db), device_id_type=MESH)
    for copy in load_own:
        copy.wait()

    ids_own = column_of(ids_in[...].astype(F32), block)
    cot_round[...] = jnp.broadcast_to(column_of(cot_in[...], block), cot_round.shape).astype(BF16)
    cot_own = cot_round[...].astype(F32)[:, 0:1]

    @pl.loop(0, wsrc.shape[0])
    def _(index):
        span = pl.ds(pl.multiple_of(index * cols, 128), cols)
        weight = jnp.broadcast_to(table[0:1, span], (block, cols))
        for c in range(1, table.shape[0]):
            weight = jnp.where(ids_own == float(c), table[c : c + 1, span], weight)
        value = weight * own[:, span].astype(F32)
        wsrc[index] = jnp.concatenate([value[:, :half], value[:, half:]], axis=0).astype(BF16)

    lane8 = lax.broadcasted_iota(jnp.int32, (block, 128), 1)
    metas[0] = jnp.where(lane8 < 64, ids_own, cot_own)
    pl.semaphore_wait(barrier, len(ring_f) + len(ring_p))

    exchange = {}
    z_order = sorted(range(ZZ), key=lambda dz: min(dz, ZZ - dz))
    own_copy = here(wsrc.at[g * K + k], w.at[0, 0, 0, 0])
    for dz in z_order:
        for dx in range(X):
            for dc in range(CORES):
                if (dz, dx, dc) == (0, 0, 0):
                    continue
                z2, x2, c2 = (zz + dz) % ZZ, (x + dx) % X, (core + dc) % CORES
                dest = ((z2 // A) * X + x2) * K + (z2 % A) * CORES + c2
                back = ((-dz) % ZZ, (-dc) % CORES, (-dx) % X)
                exchange.setdefault(back[0], []).append(
                    remote(wsrc.at[dest], w.at[0, back[0], back[1], back[2]], device(dz=dz, dx=dx, dc=dc))
                )

    from_b, from_y = {}, {}

    def send_y(db, dz):
        piece = PIECE[(db, 0)]
        for step in (1, 3):
            from_y[(db, (-step) % Y, dz)] = remote(
                w.at[piece, dz], w.at[PIECE[(db, (-step) % Y)], dz], device(dy=step)
            )

    own_copy.wait()
    for dz in z_order:
        for copy in exchange[dz]:
            copy.wait_recv()
        for db in range(1, B):
            from_b[((-db) % B, dz)] = remote(
                w.at[0, dz], w.at[PIECE[((-db) % B, 0)], dz], device(db=db)
            )
        send_y(0, dz)

    def sum_over(buffer, me, size, value, name):
        buffer[me] = value
        return [
            remote(buffer.at[me], buffer.at[me], device(**{name: step})) for step in range(1, size)
        ]

    def total_of(buffer, copies):
        for copy in copies:
            copy.wait_recv()
        total = buffer[0]
        for index in range(1, buffer.shape[0]):
            total = total + buffer[index]
        return total

    def reduce_core(first):
        span = pl.ds(first, B)
        return remote(s.at[1, :, :, span], r1.at[:, :, span], device(dc=1))

    def reduce_x(first, copy):
        span = pl.ds(first, B)
        copy.wait_recv()
        s[0, :, :, span] = s[0, :, :, span] + r1[:, :, span]
        return [
            remote(s.at[0, dx, :, span], r2.at[dx - 1, :, span], device(dx=dx)) for dx in range(1, X)
        ]

    def reduce_z(first, copies):
        span = pl.ds(first, B)
        for copy in copies:
            copy.wait_recv()
        total = s[0, 0, :, span]
        for index in range(X - 1):
            total = total + r2[index, :, span]
        s[0, 0, :, span] = total
        return [
            remote(s.at[0, 0, dz, span], r3.at[dz - 1, span], device(dz=dz)) for dz in range(1, ZZ)
        ]

    def score(piece):
        lhs = w[piece].reshape(FGROUP * rows, half)
        out = nt_dot(lhs, t2[...].reshape(2 * depth, half))
        out = out.reshape(ZZ, CORES, X, 2, block, 2 * depth)
        value = out[:, :, :, 0, :, :depth] + out[:, :, :, 1, :, depth:]
        for dz in range(ZZ):
            for dc in range(CORES):
                for dx in range(X):
                    s[dc, dx, dz, piece] = value[dz, dc, dx]

    orients = 128 * orient_rows
    orient_own = orient_in[...].astype(F32)
    orient_own = jnp.concatenate([orient_own, orient_own], axis=1)
    bin_id = lax.broadcasted_iota(jnp.int32, (orients, 128), 0).astype(F32)
    level = jnp.concatenate(
        [column_of(log_prior[index : index + 1, :], 128) for index in range(orient_rows)], axis=0
    )
    terms = jnp.sum(jnp.where(bin_id == orient_own, level, 0.0), axis=0, keepdims=True)
    sub8 = lax.broadcasted_iota(jnp.int32, (8, 128), 0)
    tmetas[k] = jnp.where(sub8 == 0, terms, orient_own)
    exchange_t, exchange_tm = [], []
    for da, dc in ring_k:
        dev, k2 = device_k(da, dc)
        for q in range(2):
            start = pl.multiple_of((g * K + k2) * cols + q * half, 128)
            exchange_t.append(remote(templates.at[:, pl.ds(start, half)], t2.at[q, k], dev))
        exchange_tm.append(remote(tmetas.at[k], tmetas.at[k], dev))
    exchange_m = [
        remote(metas.at[0], metas.at[PIECE[((-db) % B, (-dy) % Y)]], device(dy=dy, db=db)) for db, dy in ring_p
    ]

    far = {}

    def send_far(db, dz):
        for side, step in ((0, 1), (1, 3)):
            source = (-step) % Y
            from_y[(db, source, dz)].wait_recv()
            far[(db, dz, side)] = remote(
                w.at[PIECE[(db, source)], dz, side], w.at[PIECE[(db, 2)], dz, side], device(dy=step)
            )

    across = {}
    for dz in z_order:
        send_far(0, dz)
        from_b[(1, dz)].wait_recv()
        if dz not in Y_FIRST:
            send_y(1, dz)
        if dz in Y_FIRST:
            for dy in (1, 3):
                across[(dy, dz)] = remote(
                    w.at[PIECE[(0, dy)], dz], w.at[PIECE[(1, dy)], dz], device(db=1)
                )

    for copy in load_t:
        copy.wait()
    for copy in exchange_t + exchange_tm + exchange_m:
        copy.wait_recv()
    square = table[:, pl.ds(mine, cols)]
    square = square * square
    norm_part = jnp.zeros((square.shape[0], depth), F32)
    for q in range(2):
        wide = t2[q].reshape(depth, half).astype(F32)
        norm_part += nt_dot(square[:, q * half : (q + 1) * half], wide * wide, HIGH)
    norm_copies = sum_over(nz, zz, ZZ, norm_part, "dz")

    stage = [None] * len(GROUPS)
    for db in range(B):
        score(PIECE[(db, 0)])
    stage[0] = reduce_core(GROUPS[0])
    for dy in (1, 3):
        score(PIECE[(0, dy)])
    stage[0] = reduce_x(GROUPS[0], stage[0])
    stage[1] = reduce_core(GROUPS[1])
    norm_copies = sum_over(nx, x, X, total_of(nz, norm_copies), "dx")
    for dz in z_order:
        if dz not in Y_FIRST:
            send_far(1, dz)
    for dz in Y_FIRST:
        for side in range(2):
            far[(0, dz, side)].wait_recv()
        across[(2, dz)] = remote(w.at[PIECE[(0, 2)], dz], w.at[PIECE[(1, 2)], dz], device(db=1))
    stage[1] = reduce_x(GROUPS[1], stage[1])
    stage[0] = reduce_z(GROUPS[0], stage[0])
    norm_copies = sum_over(nc, core, CORES, total_of(nx, norm_copies), "dc")
    for dy in (1, 3):
        for dz in Y_FIRST:
            across[(dy, dz)].wait_recv()
        score(PIECE[(1, dy)])
    stage[2] = reduce_core(GROUPS[2])
    stage[2] = reduce_x(GROUPS[2], stage[2])
    norms = total_of(nc, norm_copies)
    for db in range(B):
        for dz in z_order:
            if dz not in Y_FIRST:
                for side in range(2):
                    far[(db, dz, side)].wait_recv()
            elif db == 1:
                across[(2, dz)].wait_recv()
        score(PIECE[(db, 2)])
    stage[3] = reduce_core(GROUPS[3])
    stage[3].wait_recv()
    span = pl.ds(GROUPS[3], B)
    s[0, :, :, span] = s[0, :, :, span] + r1[:, :, span]
    stage[3] = [
        remote(s.at[0, dx, dz, span], r4.at[dx * ZZ + dz - 1], device(dx=dx, dz=dz))
        for dz in range(ZZ) for dx in range(X) if (dx, dz) != (0, 0)
    ]
    stage[1] = reduce_z(GROUPS[1], stage[1])
    stage[2] = reduce_z(GROUPS[2], stage[2])
    for copies in stage:
        for copy in copies:
            copy.wait_recv()
    total = s[0, 0, 0, span]
    for index in range(X * ZZ - 1):
        total = total + r4[index]
    s[0, 0, 0, span] = total
    early = PIECES - B
    value = s[0, 0, 0, :early]
    for index in range(ZZ - 1):
        value = value + r3[index]
    s[0, 0, 0, :early] = value
    scores = s[0, 0, 0]
    scores = scores.reshape(owned, depth)

    info = metas[...].reshape(owned, 128)
    ids, cot = info[:, 0:1], info[:, 64:65]
    lane1 = lax.broadcasted_iota(jnp.int32, (1, 128), 1)
    prior_row = jnp.concatenate(
        [jnp.where(lane1 < 64, tmetas[i, 0:1, :], tmetas[i + 1, 0:1, :]) for i in range(0, K, 2)], axis=1
    )
    orient_row = jnp.concatenate(
        [jnp.where(lane1 < 64, tmetas[i, 1:2, :], tmetas[i + 1, 1:2, :]) for i in range(0, K, 2)], axis=1
    )
    norm_rows = jnp.zeros((owned, depth), F32)
    for c in range(norms.shape[0]):
        norm_rows = jnp.where(ids == float(c), norms[c : c + 1, :], norm_rows)
    scores = scores - 0.5 * norm_rows + prior_row
    top = jnp.max(scores, axis=1, keepdims=True)
    total = jnp.sum(jnp.exp(scores - top), axis=1, keepdims=True)
    sub = lax.broadcasted_iota(jnp.int32, (owned, 128), 0)
    lane = lax.broadcasted_iota(jnp.int32, (owned, 128), 1)
    target = sub % block
    for index, (db, dy) in enumerate(ORDER):
        place = ((y + dy) % Y) * B + (b + db) % B
        target = target + jnp.where(sub // block == index, place * block, 0)
    eye = target == lane
    top_row = jnp.sum(jnp.where(eye, top, 0.0), axis=0, keepdims=True)
    total_row = jnp.sum(jnp.where(eye, total, 0.0), axis=0, keepdims=True)
    stats[0] = jnp.where(sub8 == 0, top_row, total_row)
    copies = [
        remote(stats.at[0], stats.at[PIECE[((-db) % B, (-dy) % Y)]], device(dy=dy, db=db)) for db, dy in ring_p
    ]
    for copy in copies:
        copy.wait_recv()
    best = stats[0, 0:1, :]
    for index in range(1, PIECES):
        best = jnp.maximum(best, stats[index, 0:1, :])
    full = jnp.zeros_like(best)
    for index in range(PIECES):
        full = full + stats[index, 1:2, :] * jnp.exp(stats[index, 0:1, :] - best)
    log_row = best + jnp.log(full)
    log_col = jnp.sum(jnp.where(eye, log_row, 0.0), axis=1, keepdims=True)
    loglik[...] = jnp.broadcast_to(log_col[0:block], (block, 128))
    probs = cot * jnp.exp(scores - log_col)
    rounded = probs.astype(BF16)
    pall[0, 0, 0] = rounded

    def send_x(dz):
        return [
            remote(pall.at[0, 0, dz], pall.at[0, (-dx) % X, dz], device(dx=dx)) for dx in range(1, X)
        ]

    on_z = {
        (-dz) % ZZ: remote(pall.at[0, 0, 0], pall.at[0, 0, (-dz) % ZZ], device(dz=dz)) for dz in range(1, ZZ)
    }
    on_x = {0: send_x(0)}
    sums = [
        jnp.sum(jnp.where(ids == float(c), probs, 0.0), axis=0, keepdims=True) for c in range(norms.shape[0])
    ]
    sum_copies = sum_over(cz, zz, ZZ, jnp.concatenate(sums, axis=0), "dz")

    far_a = (a + 1) % A
    lanes = CORES * own_t

    def expand(dc, dz, side, which):
        span = pl.ds(pl.multiple_of(which * lanes, 128), lanes)
        for dx in range(X):
            part = pall[dc, dx, dz, :, span].astype(F32).reshape(PIECES, block, lanes)
            zero = jnp.zeros_like(part)
            left = jnp.concatenate([part, zero], axis=1)
            right = jnp.concatenate([zero, part], axis=1)
            p2[side, :, dx] = jnp.concatenate([left, right], axis=2).astype(BF16)

    def add_block(dc, dz, side, first=False):
        which = far_a if side == 0 else a
        expand(dc, dz, side, which)
        count = PIECES * X * rows
        value = tn_dot(p2[side].reshape(count, 2 * lanes), w[:, dz, dc].reshape(count, half))
        gacc[side] = value if first else gacc[side] + value

    for dz in z_order[1:]:
        on_z[dz].wait_recv()
        on_x[dz] = send_x(dz)
    sum_copies = sum_over(cx, x, X, total_of(cz, sum_copies), "dx")
    on_core = {}
    for dz in z_order:
        for copy in on_x[dz]:
            copy.wait_recv()
        on_core[dz] = remote(pall.at[0, :, dz], pall.at[1, :, dz], device(dc=1))
        if dz == z_order[0]:
            sum_copies = sum_over(cc, core, CORES, total_of(cx, sum_copies), "dc")
    for dz in z_order:
        add_block(0, dz, 0, dz == z_order[0])
    sums = total_of(cc, sum_copies)
    column = jnp.sum(sums, axis=0, keepdims=True)
    bin_id = lax.broadcasted_iota(jnp.int32, (orients, depth), 0).astype(F32)
    binned = jnp.sum(jnp.where(bin_id == orient_row, column, 0.0), axis=1, keepdims=True)
    eye128 = lax.broadcasted_iota(jnp.int32, (128, 128), 0) == lax.broadcasted_iota(jnp.int32, (128, 128), 1)
    tile = jnp.zeros((8, 128), F32)
    for index in range(orient_rows):
        part = binned[index * 128 : (index + 1) * 128]
        row = jnp.sum(jnp.where(eye128, part, 0.0), axis=0, keepdims=True)
        tile = jnp.where(sub8 == index, row, tile)
    place = y * B + b
    bins[place] = tile
    bin_copies = [remote(bins.at[place], bins.at[place], device(dy=dy, db=db)) for db, dy in ring_p]

    csum[...] = sums
    for dz in z_order:
        on_core[dz].wait_recv()
        add_block(1, dz, 0)
    copies, local = [], []
    for side in range(2):
        if side == 1:
            for dc in range(CORES):
                for dz in z_order:
                    add_block(dc, dz, 1, (dc, dz) == (0, z_order[0]))
        which = far_a if side == 0 else a
        span = pl.ds(pl.multiple_of(which * lanes, 128), lanes)
        class_weight = csum[:, span]
        for q in range(2):
            correction = tn_dot(class_weight, square[:, q * half : (q + 1) * half], HIGH)
            wide = t2[q, pl.ds(which * CORES, CORES)].reshape(lanes, half).astype(F32)
            value = gacc[side, q * lanes : (q + 1) * lanes] - wide * correction
            gout[side, q] = value.astype(BF16).reshape(CORES, own_t, half)
        for q in range(2):
            place_q = pl.ds(pl.multiple_of(k * cols + q * half, 128), half)
            for dc in range(CORES):
                dest = (core + dc) % CORES
                if (side, dc) == (1, 0):
                    local.append(here(gout.at[side, q, dest], grad.at[:, place_q]))
                else:
                    dev, _ = device_k(1 - side, dc)
                    copies.append(remote(gout.at[side, q, dest], grad.at[:, place_q], dev))
    for copy in sent[: -len(copies)]:
        copy.wait_send()
    prior[...] = total_of(bins, bin_copies)
    for copy in copies:
        copy.wait_recv()
    for copy in local:
        copy.wait()
    for copy in copies:
        copy.wait_send()


def local(images, ctf_ids, cotangent, templates, template_orient, ctf_table, log_prior):
    classes, width = ctf_table.shape
    orients = log_prior.shape[0]
    own_rows, own_t = images.shape[0], templates.shape[0]
    slices = ZH * X * K
    half = width // slices // 2
    rows = 2 * own_rows
    lanes = CORES * own_t
    depth = K * own_t
    cols = 2 * half
    vmem, anywhere = pl.BlockSpec(memory_space=pltpu.VMEM), pl.BlockSpec(memory_space=pl.ANY)
    grad, loglik, prior = pl.pallas_call(
        kernel,
        out_shape=(
            jax.ShapeDtypeStruct((own_t, K * cols), BF16),
            jax.ShapeDtypeStruct((own_rows, 128), F32),
            jax.ShapeDtypeStruct((8, 128), F32),
        ),
        in_specs=[pl.BlockSpec(memory_space=pltpu.HBM)] * 7,
        out_specs=(anywhere, vmem, vmem),
        scratch_shapes=[
            pltpu.VMEM((own_rows, width), BF16),
            pltpu.VMEM((classes, width), F32),
            pltpu.VMEM((1, own_rows), jnp.int32),
            pltpu.VMEM((1, own_rows), F32),
            pltpu.VMEM((1, own_t), jnp.int32),
            pltpu.VMEM((orients // 128, 128), F32),
            pltpu.VMEM((own_rows, 128), BF16),
            pltpu.VMEM((slices, rows, half), BF16),
            pltpu.VMEM((PIECES, ZZ, CORES, X, rows, half), BF16),
            pltpu.VMEM((CORES, X, ZZ, PIECES, own_rows, depth), F32),
            pltpu.VMEM((X, ZZ, PIECES, own_rows, depth), F32),
            pltpu.VMEM((X - 1, ZZ, PIECES - B, own_rows, depth), F32),
            pltpu.VMEM((ZZ - 1, PIECES - B, own_rows, depth), F32),
            pltpu.VMEM((X * ZZ - 1, B, own_rows, depth), F32),
            pltpu.VMEM((2, K, own_t, half), BF16),
            pltpu.VMEM((PIECES, own_rows, 128), F32),
            pltpu.VMEM((K, 8, 128), F32),
            pltpu.VMEM((ZZ, 8, depth), F32),
            pltpu.VMEM((X, 8, depth), F32),
            pltpu.VMEM((CORES, 8, depth), F32),
            pltpu.VMEM((ZZ, 8, depth), F32),
            pltpu.VMEM((X, 8, depth), F32),
            pltpu.VMEM((CORES, 8, depth), F32),
            pltpu.VMEM((8, depth), F32),
            pltpu.VMEM((PIECES, 8, 128), F32),
            pltpu.VMEM((PIECES, 8, 128), F32),
            pltpu.VMEM((CORES, X, ZZ, PIECES * own_rows, depth), BF16),
            pltpu.VMEM((2, PIECES, X, rows, 2 * lanes), BF16),
            pltpu.VMEM((2, 2 * lanes, half), F32),
            pltpu.VMEM((2, 2, CORES, own_t, half), BF16),
            pltpu.SemaphoreType.DMA((400,)),
        ],
        compiler_params=pltpu.CompilerParams(
            collective_id=0, has_side_effects=True, vmem_limit_bytes=56 * 1024 * 1024
        ),
        cost_estimate=pl.CostEstimate(flops=4 * 10**9, bytes_accessed=4 * 10**6, transcendentals=0),
    )(
        images,
        ctf_ids.reshape(1, own_rows),
        cotangent.reshape(1, own_rows),
        templates,
        template_orient.reshape(1, own_t),
        ctf_table,
        log_prior.reshape(orients // 128, 128),
    )
    return grad, loglik[:, 0], prior[: orients // 128].reshape(orients)


def solution(mesh):
    placed = (
        P(("tmpl", "img"), None),
        P(("tmpl", "img")),
        P(("tmpl", "img")),
        P("tmpl", None),
        P("tmpl"),
        P(),
        P(),
    )
    return jax.shard_map(
        local,
        mesh=mesh,
        in_specs=placed,
        out_specs=(P("tmpl", "img"), P(("tmpl", "img")), P()),
        check_vma=False,
    )
```
